256 devices in a mesh: member: 2 (over core), node: 32 (over z, x), tensor: 4 (over y).
Axes of the slice: x: 4, y: 4, z: 8, core: 2. Of those that a mesh axis runs over, the one named last changes fastest.
Arguments:
- layer_in: bfloat16 [131072, 512], P(('member', 'node', 'tensor')), parts along dimension 0, may hold values from -6 to 6
- output_gradient: bfloat16 [131072, 512], P(('member', 'node', 'tensor')), parts along dimension 0, may hold values from -6 to 6
- attention_gain: float32 [512], replicated, may hold values from 0.5 to 1.5
- feedforward_gain: float32 [512], replicated, may hold values from 0.5 to 1.5
- w_query: bfloat16 [512, 512], replicated, may hold values from -1.3258252 to 1.3258252
- w_key: bfloat16 [512, 512], replicated, may hold values from -1.41421356 to 1.41421356
- w_value: bfloat16 [512, 512], replicated, may hold values from -0.25 to 0.25
- w_out: bfloat16 [512, 512], replicated, may hold values from -0.25 to 0.25
- w_up: bfloat16 [512, 2048], P(None, 'tensor'), may hold values from -0.25 to 0.25
- w_down: bfloat16 [2048, 512], P('tensor'), may hold values from -0.125 to 0.125
- neighbours: int32 [512, 8], P(('node', 'tensor')), may hold values from 0 to 511, as said below
- counts: int32 [512], P(('node', 'tensor')), may hold values from 3 to 8, as said below
- node_mask: int32 [512, 128], replicated, may hold values from 0 to 1, as said below
Outputs:
- grad_in: bfloat16 [131072, 512], P(('member', 'node', 'tensor')), parts along dimension 0
The draws below stay inside these ranges and needn't reach their ends.
There are 2 independent parts, one for each index of `member`. The reference program is written for one: setup_inputs(seed, part) draws one part's arguments, and reference() takes and returns one part's arrays. A program takes and returns all parts, laid end to end along the dimension named above; an argument that names none is the same for every part. Nothing has to cross between parts.
Inputs may be any that keep to these rules, and one draw needn't show every extreme that they name: `neighbours`: slot 0 of row b is b itself; slots below counts[b] hold distinct blocks whose index differs from b by at most 4; slots from counts[b] on hold b and are ignored. `counts`: 8 is reached in every draw. `node_mask`: in each block the live nodes come first, at least 64 of them.
All inputs are finite; a program needn't handle non-finite values.
Results may differ from the reference program's by a relative error of at most 0.015.
The reference program's roundings to bfloat16 on the way count: a program that leaves them out, or rounds other values in their place, can miss the bound.
Values may be sent and summed in bfloat16 or wider, within the bound.
A program may use at most 256 MiB of HBM per device.

```python
import jax
import jax.numpy as jnp
from jax import lax

D = 512
HEADS = 8
HEAD_DIM = 64
FF = 2048
BLOCK = 128
NBR = 8
SPAN = 4
BLK_DEV = 4
NBLK = 512
NODES = 65536


def draw_w_query(key, part):
    key = jax.random.fold_in(key, 11)
    own = jnp.clip(jax.random.normal(key, (D, D), jnp.float32), -5.0, 5.0)
    return (own * D ** (-0.5)).astype(jnp.bfloat16)


def draw_w_key(key, part):
    key = jax.random.fold_in(key, 12)
    own = jnp.clip(jax.random.normal(key, (D, D), jnp.float32), -5.0, 5.0)
    return (own * D ** (-0.5)).astype(jnp.bfloat16)


def block_graph(key):
    blocks = jnp.arange(NBLK, dtype=jnp.int32)
    offsets = jnp.concatenate([jnp.arange(-SPAN, 0), jnp.arange(1, SPAN + 1)]).astype(jnp.int32)
    candidates = blocks[:, None] + offsets[None, :]
    inside = (candidates >= 0) & (candidates < NBLK)
    tiebreak = jnp.arange(2 * SPAN, dtype=jnp.int32)[None, :]
    ranking = jax.random.randint(jax.random.fold_in(key, 601), candidates.shape, 0, 1 << 20) * 64 + tiebreak
    ranking = jnp.where(inside, ranking, (1 << 27) + tiebreak)
    ordering = jnp.argsort(ranking, axis=1)
    chosen = jnp.take_along_axis(candidates, ordering[:, :NBR - 1], axis=1)
    wanted = jax.random.randint(jax.random.fold_in(key, 602), (NBLK,), 3, NBR + 1)
    chosen_slot = jax.random.randint(jax.random.fold_in(key, 603), (NBLK // BLK_DEV,), 0, BLK_DEV)
    forced = blocks % BLK_DEV == jnp.repeat(chosen_slot, BLK_DEV)
    wanted = jnp.where(forced, NBR, wanted)
    valid_count = jnp.minimum(wanted, 1 + jnp.sum(inside.astype(jnp.int32), axis=1))
    listed = jnp.concatenate([blocks[:, None], chosen], axis=1)
    listed = jnp.where(jnp.arange(NBR, dtype=jnp.int32)[None, :] < valid_count[:, None], listed, blocks[:, None])
    return (listed.astype(jnp.int32), valid_count.astype(jnp.int32))


def draw_neighbours(key, part):
    listed, valid_count = block_graph(key)
    return listed


def draw_counts(key, part):
    listed, valid_count = block_graph(key)
    return valid_count


def draw_node_mask(key, part):
    key = jax.random.fold_in(key, 23)
    live_count = jax.random.randint(key, (NBLK,), BLOCK // 2, BLOCK + 1)
    return (jnp.arange(BLOCK, dtype=jnp.int32)[None, :] < live_count[:, None]).astype(jnp.int32)


def level_of(stream_key, extent, shards, smallest, top_value):
    level, own = 1.0, jax.random.fold_in(stream_key, 6)
    for position, parts in shards:
        heights = jnp.exp(jax.random.uniform(jax.random.fold_in(own, position), (parts,), jnp.float32, smallest / len(shards), top_value / len(shards)))
        level = level * jnp.repeat(heights, extent[position] // parts).reshape([-1 if axis == position else 1 for axis in range(len(extent))])
    return level


def bell_draw(own_key, dims, width, reach, pieces=(), kind=jnp.bfloat16):
    loudness = level_of(own_key, dims, pieces, -0.22, 0.18) if pieces else 1.0
    values = jax.random.normal(own_key, dims, jnp.float32) * width * loudness
    return jnp.minimum(jnp.maximum(values, -reach), reach).astype(kind)


def setup_inputs(seed: int = 0, part: int = 0) -> dict:
    splits = jax.random.split(jax.random.key(seed), 14)
    own_keys = jax.random.split(jax.random.fold_in(splits[13], part), 14)
    return {
        "layer_in": bell_draw(own_keys[0], (NODES, D), 1.0, 6.0, ((0, 128),)),
        "output_gradient": bell_draw(own_keys[1], (NODES, D), 1.0, 6.0, ((0, 128),)),
        "attention_gain": jnp.clip(1.0 + 0.1 * jax.random.normal(splits[2], (D,), jnp.float32), 0.5, 1.5),
        "feedforward_gain": jnp.clip(1.0 + 0.1 * jax.random.normal(splits[3], (D,), jnp.float32), 0.5, 1.5),
        "w_query": draw_w_query(jax.random.fold_in(splits[13], 71), part),
        "w_key": draw_w_key(jax.random.fold_in(splits[13], 71), part),
        "w_value": bell_draw(splits[6], (D, D), D ** -0.5, 0.25),
        "w_out": bell_draw(splits[7], (D, D), D ** -0.5, 0.25),
        "w_up": bell_draw(splits[8], (D, FF), D ** -0.5, 0.25, ((1, 4),)),
        "w_down": bell_draw(splits[9], (FF, D), FF ** -0.5, 0.125, ((0, 4),)),
        "neighbours": draw_neighbours(jax.random.fold_in(splits[13], 71), part),
        "counts": draw_counts(jax.random.fold_in(splits[13], 71), part),
        "node_mask": draw_node_mask(jax.random.fold_in(splits[13], 71), part),
    }


NORM_EPS = 1e-05
GELU_C = 0.7978845608028654
GELU_A = 0.044715

def norm_apply_step(values, gain):
    centre = lax.optimization_barrier(jnp.mean(values, axis=-1, keepdims=True))
    centred = values - centre
    inverse = lax.rsqrt(lax.optimization_barrier(jnp.mean(centred * centred, axis=-1, keepdims=True)) + NORM_EPS)
    normed = centred * inverse
    return ((normed * gain).astype(jnp.bfloat16), normed, inverse)

def norm_reverse_step(upstream, normed, inverse, gain):
    scaled = upstream * gain
    first_mean = lax.optimization_barrier(jnp.mean(scaled, axis=-1, keepdims=True))
    second_mean = lax.optimization_barrier(jnp.mean(scaled * normed, axis=-1, keepdims=True))
    return inverse * (scaled - first_mean - normed * second_mean)

def gelu_slope(pre_act):
    inner = GELU_C * (pre_act + GELU_A * pre_act ** 3)
    tangent = jnp.tanh(inner)
    return 0.5 * (1.0 + tangent) + 0.5 * pre_act * (1.0 - tangent * tangent) * GELU_C * (1.0 + 3.0 * GELU_A * pre_act * pre_act)

def head_split(matrix):
    return matrix.reshape(matrix.shape[0], HEADS, HEAD_DIM).astype(jnp.float32)

def block_probs(query, key_rows, valid):
    scores = jnp.einsum('qhd,khd->hqk', head_split(query), head_split(key_rows), precision=lax.Precision.HIGHEST) * HEAD_DIM ** (-0.5)
    scores = jnp.where(valid[None, None, :], scores, -1e+30)
    top_score = lax.optimization_barrier(jnp.max(scores, axis=-1, keepdims=True))
    expo = jnp.exp(scores - top_score)
    return expo / lax.optimization_barrier(jnp.sum(expo, axis=-1, keepdims=True))

def reference(layer_in, output_gradient, attention_gain, feedforward_gain, w_query, w_key, w_value, w_out, w_up, w_down, neighbours, counts, node_mask):
    input_float_rows = layer_in.astype(jnp.float32)
    first_normed_rows, first_centred_scaled, first_inverse_norm = norm_apply_step(input_float_rows, attention_gain)
    queries = jnp.dot(first_normed_rows, w_query, preferred_element_type=jnp.float32).astype(jnp.bfloat16)
    key_all = jnp.dot(first_normed_rows, w_key, preferred_element_type=jnp.float32).astype(jnp.bfloat16)
    value_all = jnp.dot(first_normed_rows, w_value, preferred_element_type=jnp.float32).astype(jnp.bfloat16)
    key_blocks = key_all.reshape(NBLK, BLOCK, D)
    value_blocks = value_all.reshape(NBLK, BLOCK, D)
    query_blocks = queries.reshape(NBLK, BLOCK, D)
    slot_ok = jnp.arange(NBR, dtype=jnp.int32)[None, :] < counts[:, None]
    live_keys = (node_mask[neighbours] > 0) & slot_ok[:, :, None]

    def attend(packed):
        query, block_ids, valid = packed
        near_keys = key_blocks[block_ids].reshape(NBR * BLOCK, D)
        near_values = value_blocks[block_ids].reshape(NBR * BLOCK, D)
        weights = block_probs(query, near_keys, valid.reshape(-1)).astype(jnp.bfloat16)
        mixed = jnp.einsum('hqk,khd->qhd', weights.astype(jnp.float32), head_split(near_values), precision=lax.Precision.HIGHEST)
        return mixed.reshape(BLOCK, D).astype(jnp.bfloat16)
    attended = lax.map(attend, (query_blocks, neighbours, live_keys)).reshape(NODES, D)
    middle_state = input_float_rows + jnp.dot(attended, w_out, preferred_element_type=jnp.float32)
    second_normed_rows, second_centred_scaled, second_inverse_norm = norm_apply_step(middle_state, feedforward_gain)
    pre_act = jnp.dot(second_normed_rows, w_up, preferred_element_type=jnp.float32)
    grad_mid = jnp.dot(output_gradient, w_down.T, preferred_element_type=jnp.float32)
    grad_act = (grad_mid * gelu_slope(pre_act)).astype(jnp.bfloat16)
    second_norm_gradient = jnp.dot(grad_act, w_up.T, preferred_element_type=jnp.float32)
    residual_middle_gradient = output_gradient.astype(jnp.float32) + norm_reverse_step(second_norm_gradient, second_centred_scaled, second_inverse_norm, feedforward_gain)
    grad_attended = jnp.dot(residual_middle_gradient.astype(jnp.bfloat16), w_out.T, preferred_element_type=jnp.float32).astype(jnp.bfloat16)
    grad_blocks = grad_attended.reshape(NBLK, BLOCK, D)

    def backward(totals, packed):
        query, block_ids, valid, upstream = packed
        near_keys = key_blocks[block_ids].reshape(NBR * BLOCK, D)
        near_values = value_blocks[block_ids].reshape(NBR * BLOCK, D)
        probs = block_probs(query, near_keys, valid.reshape(-1))
        weights = probs.astype(jnp.bfloat16)
        upstream_heads = head_split(upstream)
        grad_prob = jnp.einsum('qhd,khd->hqk', upstream_heads, head_split(near_values), precision=lax.Precision.HIGHEST)
        centre = lax.optimization_barrier(jnp.sum(probs * grad_prob, axis=-1, keepdims=True))
        grad_score = (probs * (grad_prob - centre) * HEAD_DIM ** (-0.5)).astype(jnp.bfloat16)
        grad_query = jnp.einsum('hqk,khd->qhd', grad_score.astype(jnp.float32), head_split(near_keys), precision=lax.Precision.HIGHEST)
        grad_keys = jnp.einsum('hqk,qhd->khd', grad_score.astype(jnp.float32), head_split(query), precision=lax.Precision.HIGHEST)
        grad_values = jnp.einsum('hqk,qhd->khd', weights.astype(jnp.float32), upstream_heads, precision=lax.Precision.HIGHEST)
        stacked = jnp.stack([grad_keys.reshape(NBR, BLOCK, D), grad_values.reshape(NBR, BLOCK, D)], axis=1)
        totals = totals.at[block_ids].add(stacked)
        return (totals, grad_query.reshape(BLOCK, D).astype(jnp.bfloat16))
    start_totals = jnp.zeros((NBLK, 2, BLOCK, D), jnp.float32)
    totals, grad_query_blocks = lax.scan(backward, start_totals, (query_blocks, neighbours, live_keys, grad_blocks))
    grad_queries = grad_query_blocks.reshape(NODES, D)
    grad_keys_all = totals[:, 0].reshape(NODES, D).astype(jnp.bfloat16)
    grad_values_all = totals[:, 1].reshape(NODES, D).astype(jnp.bfloat16)
    first_norm_gradient = jnp.dot(grad_queries, w_query.T, preferred_element_type=jnp.float32) + jnp.dot(grad_keys_all, w_key.T, preferred_element_type=jnp.float32) + jnp.dot(grad_values_all, w_value.T, preferred_element_type=jnp.float32)
    return (residual_middle_gradient + norm_reverse_step(first_norm_gradient, first_centred_scaled, first_inverse_norm, attention_gain)).astype(jnp.bfloat16)
```

```python
import functools

import jax
import jax.numpy as jnp
from jax import lax
from jax.experimental import pallas as pl
from jax.experimental.pallas import tpu as pltpu
from jax.sharding import PartitionSpec as P

HEADS = 8
HEAD_DIM = 64
NBR = 8
SPAN = 4
BLK = 128
OWN = 4
EXT = OWN + 2 * SPAN
WIN = 2 * SPAN + 1
GRP = 4
SLAB = GRP * HEAD_DIM
NGRP = HEADS // GRP
STK = GRP * BLK
NIT = OWN * NGRP

NORM_EPS = 1e-05
GELU_C = 0.7978845608028654
GELU_A = 0.044715
FAR = -1e30

f32 = jnp.float32
bf16 = jnp.bfloat16
MESH = pl.DeviceIdType.MESH


def dot(left, right):
    return jnp.dot(left, right, preferred_element_type=f32)


def dot_last(left, right):
    return lax.dot_general(left, right, (((1,), (1,)), ((), ())), preferred_element_type=f32)


def norm_parts(values):
    centre = jnp.mean(values, axis=-1, keepdims=True)
    centred = values - centre
    inverse = lax.rsqrt(jnp.mean(centred * centred, axis=-1, keepdims=True) + NORM_EPS)
    return centred * inverse, inverse


def norm_reverse(upstream, normed, inverse, gain):
    scaled = upstream * gain
    first = jnp.mean(scaled, axis=-1, keepdims=True)
    second = jnp.mean(scaled * normed, axis=-1, keepdims=True)
    return inverse * (scaled - first - normed * second)


def gelu_slope(v):
    square = v * v
    tangent = jnp.tanh(v * (GELU_C + GELU_C * GELU_A * square))
    return 0.5 * (1.0 + tangent) + (0.5 * v) * (1.0 - tangent * tangent) * (
        GELU_C + 3.0 * GELU_C * GELU_A * square
    )


def lanes4(tile):
    return jnp.concatenate([tile] * GRP, axis=1)


def put_stack(dst, index, slab):
    head = lax.broadcasted_iota(jnp.int32, (BLK, SLAB), 1) // HEAD_DIM
    for h in range(GRP):
        dst[index, h * BLK : (h + 1) * BLK, :] = jnp.where(head == h, slab, 0.0).astype(bf16)


def diagonal(wide):
    return jnp.concatenate(
        [
            wide[h * HEAD_DIM : (h + 1) * HEAD_DIM, h * BLK : (h + 1) * BLK]
            for h in range(GRP)
        ],
        axis=0,
    )


def kernel(
    nodes,
    tensors,
    x_ref,
    og_ref,
    ag_ref,
    fg_ref,
    wq_ref,
    wk_ref,
    wv_ref,
    wo_ref,
    wu_hbm,
    wd_hbm,
    nbr_ref,
    cnt_ref,
    nm_ref,
    out_ref,
    halo,
    n1h,
    qm,
    qmr,
    kext,
    vext,
    ktr,
    vtr,
    live,
    vsc,
    vbs,
    vbr,
    wbuf,
    sbuf,
    ebuf,
    att,
    attt,
    stats,
    statr,
    invs,
    mid,
    n2,
    acc,
    gmr,
    dob,
    dor,
    dom,
    domr,
    dsb,
    dq,
    dk,
    dv,
    send,
    recv,
    local,
):
    member = lax.axis_index("member")
    node = lax.axis_index("node")
    tensor = lax.axis_index("tensor")
    total = nodes * tensors
    place = node * tensors + tensor
    after = lax.rem(place + 1, total)
    before = lax.rem(place + total - 1, total)
    right = (member, after // tensors, lax.rem(after, tensors))
    left = (member, before // tensors, lax.rem(before, tensors))
    up = (member, node, lax.rem(tensor + 1, tensors))
    down = (member, node, lax.rem(tensor + tensors - 1, tensors))
    twin = (1 - member, node, tensor)

    barrier = pltpu.get_barrier_semaphore()
    for peer in (right, left, up, down, twin):
        pl.semaphore_signal(barrier, inc=1, device_id=peer, device_id_type=MESH)
    pl.semaphore_wait(barrier, 5)

    def copy(slot, src, dst, peer):
        return pltpu.make_async_remote_copy(
            src_ref=src,
            dst_ref=dst,
            send_sem=send.at[slot],
            recv_sem=recv.at[slot],
            device_id=peer,
            device_id_type=MESH,
        )

    rows_right = copy(0, x_ref, halo.at[0], right)
    rows_left = copy(1, x_ref, halo.at[1], left)
    rows_right.start()
    rows_left.start()
    own_up = pltpu.make_async_copy(wu_hbm, wbuf.at[0, 0], local.at[0])
    own_down = pltpu.make_async_copy(wd_hbm, wbuf.at[0, 1], local.at[1])
    own_up.start()
    own_down.start()

    def valid_row(b, carry):
        def valid_one(c, carry):
            wanted = place * OWN - SPAN + b + c
            hit = jnp.int32(0)
            for j in range(NBR):
                same = (nbr_ref[b, j] == wanted) & (j < cnt_ref[b])
                hit = hit | same.astype(jnp.int32)
            vsc[b * WIN + c] = jnp.where(hit > 0, 0.0, FAR).astype(f32)
            return carry

        return lax.fori_loop(0, WIN, valid_one, carry)

    lax.fori_loop(0, OWN, valid_row, 0)
    for b in range(OWN):
        for e in range(OWN):
            row = b * OWN + e
            low = vsc[b * WIN + e - b] if e >= b else jnp.float32(FAR)
            high = vsc[b * WIN + e - b + 2 * SPAN] if e <= b else jnp.float32(FAR)
            vbs[0, row : row + 1, :] = jnp.full((1, BLK), low, f32)
            vbs[1, row : row + 1, :] = jnp.full((1, BLK), high, f32)
    lists_right = copy(2, vbs.at[1], vbr.at[0], right)
    lists_left = copy(3, vbs.at[0], vbr.at[1], left)
    lists_right.start()
    lists_left.start()

    for e in range(EXT):
        block = jnp.clip(place * OWN - SPAN + e, 0, total * OWN - 1)
        line = jnp.where(nm_ref[pl.ds(block, 1), :] > 0, 0.0, FAR).astype(f32)
        live[e * BLK : (e + 1) * BLK, :] = jnp.broadcast_to(line, (BLK, BLK)).T

    def keys_values(normed, base):
        rows = normed.shape[0]
        base = pl.multiple_of(base, BLK)
        k = dot(normed, wk_ref[...]).astype(bf16)
        v = dot(normed, wv_ref[...]).astype(bf16)
        for g in range(NGRP):
            kg, vg = k[:, g * SLAB : (g + 1) * SLAB], v[:, g * SLAB : (g + 1) * SLAB]
            kext[g, pl.ds(base, rows), :] = kg
            vext[g, pl.ds(base, rows), :] = vg
            ktr[g, :, pl.ds(base, rows)] = kg.T
            vtr[g, :, pl.ds(base, rows)] = vg.T

    def queries(normed, dst, first):
        q = dot(normed, wq_ref[...]).astype(bf16).astype(f32) * HEAD_DIM ** (-0.5)
        for i in range(normed.shape[0] // BLK):
            for g in range(NGRP):
                put_stack(
                    dst,
                    first + i * NGRP + g,
                    q[i * BLK : (i + 1) * BLK, g * SLAB : (g + 1) * SLAB],
                )

    def own_rows(r, carry):
        base = pl.multiple_of(r * 256, 256)
        normed, _ = norm_parts(x_ref[pl.ds(base, 256), :].astype(f32))
        normed = (normed * ag_ref[...]).astype(bf16)
        keys_values(normed, SPAN * BLK + base)
        queries(normed, qm, r * 2 * NGRP)
        return carry

    lax.fori_loop(0, 2, own_rows, 0)

    rows_right.wait_recv()
    rows_left.wait_recv()
    rows_right.wait_send()
    rows_left.wait_send()

    own_up.wait()
    own_down.wait()
    ring_up = copy(4, wbuf.at[0, member], wbuf.at[1, member], up)
    ring_down = copy(5, wbuf.at[0, member], wbuf.at[2, member], down)
    ring_up.start()
    ring_down.start()

    def halo_rows(r, carry):
        side = r // 2
        base = pl.multiple_of(lax.rem(r, 2) * 256, 256)
        normed, _ = norm_parts(halo[side, pl.ds(base, 256), :].astype(f32))
        normed = (normed * ag_ref[...]).astype(bf16)
        n1h[side, pl.ds(base, 256), :] = normed
        keys_values(normed, side * (SPAN + OWN) * BLK + base)
        return carry

    lax.fori_loop(0, 4, halo_rows, 0)

    CH = 3
    CR = CH * BLK

    def window_bias(b, c):
        base = pl.multiple_of(b * BLK, BLK)
        tiles = []
        for j in range(CH):
            tile = live[pl.ds(base + (c * CH + j) * BLK, BLK), :]
            tiles.append(tile + vsc[b * WIN + c * CH + j])
        return lanes4(jnp.concatenate(tiles, axis=0))

    def forward(it, carry):
        b, g = it // NGRP, lax.rem(it, NGRP)
        base = pl.multiple_of(b * BLK, BLK)
        stack = qm[it]
        top = jnp.full((1, STK), 2 * FAR, f32)
        for c in range(WIN // CH):
            s = dot_last(kext[g, pl.ds(base + c * CR, CR), :], stack) + window_bias(b, c)
            sbuf[c * CR : (c + 1) * CR, :] = s
            top = jnp.maximum(top, jnp.max(s, axis=0, keepdims=True))
        count = jnp.zeros((1, STK), f32)
        for c in range(WIN // CH):
            e = jnp.exp(sbuf[c * CR : (c + 1) * CR, :] - top)
            count = count + jnp.sum(e, axis=0, keepdims=True)
            ebuf[it, c * CR : (c + 1) * CR, :] = e.astype(bf16)
        inverse = 1.0 / count
        wide = dot(vtr[g, :, pl.ds(base, WIN * BLK)], ebuf[it]) * inverse
        own = diagonal(wide)
        attt[it] = own
        att[g, pl.ds(base, BLK), :] = own.T.astype(bf16)
        stats[pl.ds(it, 1), :] = top + jnp.log(count)
        invs[pl.ds(it, 1), :] = inverse
        return carry

    lax.fori_loop(0, 6, forward, 0)

    ring_up.wait_recv()
    ring_down.wait_recv()
    cross_up = copy(
        6, wbuf.at[1, member, pl.ds(0, 256)], wbuf.at[3, member, pl.ds(0, 256)], up
    )
    cross_down = copy(
        7, wbuf.at[2, member, pl.ds(256, 256)], wbuf.at[3, member, pl.ds(256, 256)], down
    )
    cross_up.start()
    cross_down.start()
    twin_one = copy(8, wbuf.at[1, member], wbuf.at[1, member], twin)
    twin_two = copy(9, wbuf.at[2, member], wbuf.at[2, member], twin)
    twin_one.start()
    twin_two.start()

    lax.fori_loop(6, NIT, forward, 0)

    def middle(r, carry):
        rows = pl.ds(pl.multiple_of(r * 256, 256), 256)
        value = x_ref[rows, :].astype(f32) + (
            dot(att[0, rows, :], wo_ref[0:SLAB, :]) + dot(att[1, rows, :], wo_ref[SLAB:, :])
        )
        mid[rows, :] = value
        normed, _ = norm_parts(value)
        n2[rows, :] = (normed * fg_ref[...]).astype(bf16)
        acc[rows, :] = jnp.zeros((256, acc.shape[1]), f32)
        return carry

    lax.fori_loop(0, 2, middle, 0)

    def hidden(slot):
        def run(r, carry):
            rows = pl.ds(pl.multiple_of(r * 256, 256), 256)
            pre = dot(n2[rows, :], wbuf[slot, 0])
            slope = gelu_slope(pre)
            grad = dot_last(og_ref[rows, :], wbuf[slot, 1])
            act = (grad * slope).astype(bf16)
            acc[rows, :] += dot_last(act, wbuf[slot, 0])
            return carry

        lax.fori_loop(0, 2, run, 0)

    other = 1 - member

    def arrival(slot_id, slot, part):
        return copy(slot_id, wbuf.at[slot, other, part], wbuf.at[slot, other, part], twin)

    hidden(0)
    arrival(8, 1, pl.ds(0, 512)).wait_recv()
    hidden(1)
    cross_up.wait_recv()
    cross_down.wait_recv()
    twin_three = copy(10, wbuf.at[3, member], wbuf.at[3, member], twin)
    twin_three.start()
    arrival(9, 2, pl.ds(0, 512)).wait_recv()
    hidden(2)
    arrival(10, 3, pl.ds(0, 512)).wait_recv()
    hidden(3)

    for b in range(OWN):
        rows = slice(b * BLK, (b + 1) * BLK)
        up_grad = og_ref[rows, :].astype(f32)
        normed, inverse = norm_parts(mid[rows, :])
        res = up_grad + norm_reverse(acc[rows, :], normed, inverse, fg_ref[...])
        gmr[rows, :] = res
        res_bf = res.astype(bf16)
        n2[rows, :] = res_bf
        grad_att = dot_last(res_bf, wo_ref[...]).astype(bf16)
        dob[rows, :] = grad_att
        grad_wide = grad_att.astype(f32)
        grad_t = dot_last(wo_ref[...], res_bf).astype(bf16).astype(f32)
        for g in range(NGRP):
            it = b * NGRP + g
            put_stack(dom, it, grad_wide[:, g * SLAB : (g + 1) * SLAB])
            product = grad_t[g * SLAB : (g + 1) * SLAB, :] * attt[it]
            stats[NIT + it : NIT + it + 1, :] = jnp.concatenate(
                [
                    jnp.sum(product[h * HEAD_DIM : (h + 1) * HEAD_DIM], axis=0, keepdims=True)
                    for h in range(GRP)
                ],
                axis=1,
            )

    grads_right = copy(11, dob, dor.at[0], right)
    grads_left = copy(12, dob, dor.at[1], left)
    stats_right = copy(13, stats, statr.at[0], right)
    stats_left = copy(14, stats, statr.at[1], left)
    stats_right.start()
    stats_left.start()
    grads_right.start()
    grads_left.start()

    dk[...] = jnp.zeros(dk.shape, f32)
    dv[...] = jnp.zeros(dv.shape, f32)

    def backward(it, carry):
        b, g = it // NGRP, lax.rem(it, NGRP)
        base = pl.multiple_of(b * BLK, BLK)
        grad_stack = dom[it]
        inverse = invs[pl.ds(it, 1), :]
        centre = stats[pl.ds(NIT + it, 1), :]
        for c in range(WIN // CH):
            rows = slice(c * CR, (c + 1) * CR)
            grad_prob = dot_last(vext[g, pl.ds(base + c * CR, CR), :], grad_stack)
            probs = ebuf[it, rows, :].astype(f32) * inverse
            ebuf[it, rows, :] = probs.astype(bf16)
            dsb[rows, :] = (probs * (grad_prob - centre)).astype(bf16)
        wide = dot(ktr[g, :, pl.ds(base, WIN * BLK)], dsb[...])
        dq[g, pl.ds(base, BLK), :] = (diagonal(wide) * HEAD_DIM ** (-0.5)).T.astype(bf16)
        own = pl.ds(pl.multiple_of((SPAN - b) * BLK, BLK), OWN * BLK)
        dk[g] += dot(dsb[own, :], qm[it])
        dv[g] += dot(ebuf[it, own, :], grad_stack)
        return carry

    lax.fori_loop(0, NIT, backward, 0)

    def far_queries(r, carry):
        side = r // 2
        base = pl.multiple_of(lax.rem(r, 2) * 256, 256)
        queries(n1h[side, pl.ds(base, 256), :], qmr, r * 2 * NGRP)
        return carry

    lax.fori_loop(0, 4, far_queries, 0)

    lists_right.wait_recv()
    lists_left.wait_recv()
    stats_right.wait_recv()
    stats_left.wait_recv()
    grads_right.wait_recv()
    grads_left.wait_recv()

    for side in range(2):
        for b in range(OWN):
            for g in range(NGRP):
                put_stack(
                    domr,
                    (side * OWN + b) * NGRP + g,
                    dor[side, b * BLK : (b + 1) * BLK, g * SLAB : (g + 1) * SLAB].astype(f32),
                )

    for side in range(2):
        for b in range(OWN):
            first, last = (0, b + 1) if side == 0 else (b, OWN)

            def remote(g, carry, side=side, b=b, first=first, last=last):
                it = b * NGRP + g
                stack = qmr[side * NIT + it]
                grad_stack = domr[side * NIT + it]
                level = statr[side, pl.ds(it, 1), :]
                centre = statr[side, pl.ds(NIT + it, 1), :]
                rows = slice(first * BLK, last * BLK)
                ext = slice((SPAN + first) * BLK, (SPAN + last) * BLK)
                s = dot_last(kext[g, ext, :], stack)
                shift = []
                for c in range(first, last):
                    row = b * OWN + c
                    listed = lanes4(vbr[side, row : row + 1, :]) - level
                    part = s[(c - first) * BLK : (c - first + 1) * BLK, :]
                    shift.append(
                        part + (lanes4(live[(SPAN + c) * BLK : (SPAN + c + 1) * BLK, :]) + listed)
                    )
                probs = jnp.exp(jnp.concatenate(shift, axis=0))
                grad_prob = dot_last(vext[g, ext, :], grad_stack)
                grad_score = (probs * (grad_prob - centre)).astype(bf16)
                dk[g, rows, :] += dot(grad_score, stack)
                dv[g, rows, :] += dot(probs.astype(bf16), grad_stack)
                return carry

            lax.fori_loop(0, NGRP, remote, 0)

    def finish(r, carry):
        rows = pl.ds(pl.multiple_of(r * 256, 256), 256)
        grad = None
        for g in range(NGRP):
            cols = slice(g * SLAB, (g + 1) * SLAB)
            term = dot_last(dq[g, rows, :], wq_ref[:, cols])
            term += dot_last(dk[g, rows, :].astype(bf16), wk_ref[:, cols])
            term += dot_last(dv[g, rows, :].astype(bf16), wv_ref[:, cols])
            grad = term if grad is None else grad + term
        normed, inverse = norm_parts(x_ref[rows, :].astype(f32))
        out_ref[rows, :] = (
            gmr[rows, :] + norm_reverse(grad, normed, inverse, ag_ref[...])
        ).astype(out_ref.dtype)
        return carry

    lax.fori_loop(0, 2, finish, 0)

    for done in (
        lists_right,
        lists_left,
        ring_up,
        ring_down,
        cross_up,
        cross_down,
        twin_one,
        twin_two,
        twin_three,
        stats_right,
        stats_left,
        grads_right,
        grads_left,
    ):
        done.wait_send()


def body(nodes, tensors, *args):
    (x, og, ag, fg, wq, wk, wv, wo, wu, wd, nbr, cnt, nm) = args
    rows, width = x.shape
    vm = pl.BlockSpec(memory_space=pltpu.VMEM)
    sm = pl.BlockSpec(memory_space=pltpu.SMEM)
    hbm = pl.BlockSpec(memory_space=pl.ANY)
    V = pltpu.VMEM
    return pl.pallas_call(
        functools.partial(kernel, nodes, tensors),
        out_shape=jax.ShapeDtypeStruct((rows, width), bf16),
        in_specs=[vm] * 8 + [hbm] * 2 + [sm] * 2 + [vm],
        out_specs=vm,
        scratch_shapes=[
            V((2, rows, width), bf16),
            V((2, rows, width), bf16),
            V((NIT, STK, SLAB), bf16),
            V((2 * NIT, STK, SLAB), bf16),
            V((NGRP, EXT * BLK, SLAB), bf16),
            V((NGRP, EXT * BLK, SLAB), bf16),
            V((NGRP, SLAB, EXT * BLK), bf16),
            V((NGRP, SLAB, EXT * BLK), bf16),
            V((EXT * BLK, BLK), f32),
            pltpu.SMEM((OWN * WIN,), f32),
            V((2, OWN * OWN, BLK), f32),
            V((2, OWN * OWN, BLK), f32),
            V((4, 2, width, width), bf16),
            V((WIN * BLK, STK), f32),
            V((NIT, WIN * BLK, STK), bf16),
            V((NGRP, rows, SLAB), bf16),
            V((NIT, SLAB, BLK), f32),
            V((2 * NIT, STK), f32),
            V((2, 2 * NIT, STK), f32),
            V((NIT, STK), f32),
            V((rows, width), f32),
            V((rows, width), bf16),
            V((rows, width), f32),
            V((rows, width), f32),
            V((rows, width), bf16),
            V((2, rows, width), bf16),
            V((NIT, STK, SLAB), bf16),
            V((2 * NIT, STK, SLAB), bf16),
            V((WIN * BLK, STK), bf16),
            V((NGRP, rows, SLAB), bf16),
            V((NGRP, rows, SLAB), f32),
            V((NGRP, rows, SLAB), f32),
            pltpu.SemaphoreType.DMA((15,)),
            pltpu.SemaphoreType.DMA((15,)),
            pltpu.SemaphoreType.DMA((2,)),
        ],
        compiler_params=pltpu.CompilerParams(
            collective_id=0, has_side_effects=True, vmem_limit_bytes=60 * 1024 * 1024
        ),
    )(x, og, ag.reshape(1, width), fg.reshape(1, width), wq, wk, wv, wo, wu, wd, nbr, cnt, nm)


def solution(mesh):
    return jax.shard_map(
        functools.partial(body, mesh.shape["node"], mesh.shape["tensor"]),
        mesh=mesh,
        in_specs=(
            P(("member", "node", "tensor"), None),
            P(("member", "node", "tensor"), None),
            P(),
            P(),
            P(),
            P(),
            P(),
            P(),
            P(None, "tensor"),
            P("tensor", None),
            P(("node", "tensor"), None),
            P(("node", "tensor")),
            P(),
        ),
        out_specs=P(("member", "node", "tensor"), None),
        check_vma=False,
    )
```

```python
import functools

import jax
import jax.numpy as jnp
from jax import lax
from jax.experimental import pallas as pl
from jax.experimental.pallas import tpu as pltpu
from jax.sharding import PartitionSpec as P

HEADS = 8
HEAD_DIM = 64
NBR = 8
SPAN = 4
BLK = 128
OWN = 4
HWIN = SPAN + 1
GRP = 4
SLAB = GRP * HEAD_DIM
NGRP = HEADS // GRP
STK = GRP * BLK
NIT = OWN * NGRP

NORM_EPS = 1e-05
GELU_C = 0.7978845608028654
GELU_A = 0.044715
FAR = -1e30

f32 = jnp.float32
bf16 = jnp.bfloat16
MESH = pl.DeviceIdType.MESH


def dot(left, right):
    return jnp.dot(left, right, preferred_element_type=f32)


def dot_last(left, right):
    return lax.dot_general(left, right, (((1,), (1,)), ((), ())), preferred_element_type=f32)


def norm_parts(values):
    centre = jnp.mean(values, axis=-1, keepdims=True)
    centred = values - centre
    inverse = lax.rsqrt(jnp.mean(centred * centred, axis=-1, keepdims=True) + NORM_EPS)
    return centred * inverse, inverse


def norm_reverse(upstream, normed, inverse, gain):
    scaled = upstream * gain
    first = jnp.mean(scaled, axis=-1, keepdims=True)
    second = jnp.mean(scaled * normed, axis=-1, keepdims=True)
    return inverse * (scaled - first - normed * second)


def gelu_slope(v):
    square = v * v
    tangent = jnp.tanh(v * (GELU_C + GELU_C * GELU_A * square))
    return 0.5 * (1.0 + tangent) + (0.5 * v) * (1.0 - tangent * tangent) * (
        GELU_C + 3.0 * GELU_C * GELU_A * square
    )


def lanes4(tile):
    return jnp.concatenate([tile] * GRP, axis=1)


def put_stack(dst, index, slab):
    head = lax.broadcasted_iota(jnp.int32, (BLK, SLAB), 1) // HEAD_DIM
    for h in range(GRP):
        dst[index, h * BLK : (h + 1) * BLK, :] = jnp.where(head == h, slab, 0.0).astype(bf16)


def diagonal(wide):
    return jnp.concatenate(
        [
            wide[h * HEAD_DIM : (h + 1) * HEAD_DIM, h * BLK : (h + 1) * BLK]
            for h in range(GRP)
        ],
        axis=0,
    )


def kernel(
    nodes,
    tensors,
    x_hbm,
    og_hbm,
    ag_ref,
    fg_ref,
    wq_hbm,
    wk_hbm,
    wv_hbm,
    wo_hbm,
    wu_hbm,
    wd_hbm,
    nbr_ref,
    cnt_ref,
    nm_hbm,
    out_ref,
    x_ref,
    og_ref,
    wq_ref,
    wk_ref,
    wv_ref,
    wo_ref,
    nm_ref,
    halo,
    n1h,
    qm,
    qmr,
    kown,
    vown,
    ktown,
    vtown,
    khal,
    vhal,
    kthal,
    vthal,
    live,
    vsc,
    vbs,
    vbr,
    wbuf,
    sbuf,
    eown,
    ehal,
    att,
    attt,
    top_one,
    count_one,
    lse,
    lser,
    centre,
    centrer,
    inv_own,
    inv_hal,
    mid,
    n2,
    acc,
    gmr,
    dob,
    dor,
    dom,
    domr,
    prem,
    dq,
    dk,
    dv,
    send,
    recv,
    local,
):
    member = lax.axis_index("member")
    node = lax.axis_index("node")
    tensor = lax.axis_index("tensor")
    total = nodes * tensors
    place = node * tensors + tensor
    has_left = place > 0
    has_right = place < total - 1
    after = lax.rem(place + 1, total)
    before = lax.rem(place + total - 1, total)
    right = (member, after // tensors, lax.rem(after, tensors))
    left = (member, before // tensors, lax.rem(before, tensors))
    up = (member, node, lax.rem(tensor + 1, tensors))
    down = (member, node, lax.rem(tensor + tensors - 1, tensors))
    twin = (1 - member, node, tensor)

    loads = {}
    for i, (name, src, dst) in enumerate(
        (
            ("x", x_hbm, x_ref),
            ("wk", wk_hbm, wk_ref),
            ("wv", wv_hbm, wv_ref),
            ("wq", wq_hbm, wq_ref),
            ("nm", nm_hbm, nm_ref),
            ("wu", wu_hbm, wbuf.at[0, 0]),
            ("wd", wd_hbm, wbuf.at[0, 1]),
            ("wo", wo_hbm, wo_ref),
            ("og", og_hbm, og_ref),
        )
    ):
        loads[name] = pltpu.make_async_copy(src, dst, local.at[i])
        loads[name].start()

    barrier = pltpu.get_barrier_semaphore()
    for peer in (up, down, twin):
        pl.semaphore_signal(barrier, inc=1, device_id=peer, device_id_type=MESH)

    @pl.when(has_right)
    def _():
        pl.semaphore_signal(barrier, inc=1, device_id=right, device_id_type=MESH)

    @pl.when(has_left)
    def _():
        pl.semaphore_signal(barrier, inc=1, device_id=left, device_id_type=MESH)

    pl.semaphore_wait(barrier, 3 + has_right.astype(jnp.int32) + has_left.astype(jnp.int32))

    def copy(slot, src, dst, peer):
        return pltpu.make_async_remote_copy(
            src_ref=src,
            dst_ref=dst,
            send_sem=send.at[slot],
            recv_sem=recv.at[slot],
            device_id=peer,
            device_id_type=MESH,
        )

    class Pair:
        def __init__(self, slot, to_right, to_left, dst):
            self.to_right = lambda: copy(slot, to_right, dst.at[0], right)
            self.to_left = lambda: copy(slot + 1, to_left, dst.at[1], left)

        def each(self, right_one, left_one, do):
            @pl.when(right_one)
            def _():
                do(self.to_right())

            @pl.when(left_one)
            def _():
                do(self.to_left())

        def start(self):
            self.each(has_right, has_left, lambda c: c.start())

        def wait_send(self):
            self.each(has_right, has_left, lambda c: c.wait_send())

        def wait_recv(self):
            self.each(has_left, has_right, lambda c: c.wait_recv())

    rows = Pair(0, x_hbm, x_hbm, halo)
    rows.start()

    def listed(b, wanted):
        hit = jnp.int32(0)
        for j in range(NBR):
            same = (nbr_ref[b, j] == wanted) & (j < cnt_ref[b])
            hit = hit | same.astype(jnp.int32)
        return jnp.where(hit > 0, 0.0, FAR).astype(f32)

    def valid_row(b, carry):
        for c in range(OWN):
            vsc[b * OWN + c] = listed(b, place * OWN + c)
        for j in range(HWIN):
            e = b + j
            vsc[OWN * OWN + b * HWIN + j] = listed(
                b, place * OWN + jnp.where(e < SPAN, e - SPAN, e - SPAN + OWN)
            )
        return carry

    lax.fori_loop(0, OWN, valid_row, 0)
    for b in range(OWN):
        for e in range(OWN):
            row = b * OWN + e
            base = OWN * OWN + b * HWIN
            low = vsc[base + e - b] if e >= b else jnp.float32(FAR)
            high = vsc[base + SPAN + e - b] if e <= b else jnp.float32(FAR)
            vbs[0, row : row + 1, :] = jnp.full((1, BLK), low, f32)
            vbs[1, row : row + 1, :] = jnp.full((1, BLK), high, f32)
    lists = Pair(2, vbs.at[1], vbs.at[0], vbr)
    lists.start()

    @pl.when(jnp.logical_not(has_left))
    def _():
        vbr[0] = jnp.full(vbr.shape[1:], FAR, f32)
        lser[0] = jnp.zeros(lser.shape[1:], f32)
        centrer[0] = jnp.zeros(centrer.shape[1:], f32)
        halo[0] = jnp.zeros(halo.shape[1:], bf16)
        dor[0] = jnp.zeros(dor.shape[1:], bf16)

    @pl.when(jnp.logical_not(has_right))
    def _():
        vbr[1] = jnp.full(vbr.shape[1:], FAR, f32)
        lser[1] = jnp.zeros(lser.shape[1:], f32)
        centrer[1] = jnp.zeros(centrer.shape[1:], f32)
        halo[1] = jnp.zeros(halo.shape[1:], bf16)
        dor[1] = jnp.zeros(dor.shape[1:], bf16)

    def keys_values(normed, base, k_dst, v_dst, kt_dst, vt_dst):
        count = normed.shape[0]
        base = pl.multiple_of(base, BLK)
        k = dot(normed, wk_ref[...]).astype(bf16)
        v = dot(normed, wv_ref[...]).astype(bf16)
        for g in range(NGRP):
            kg, vg = k[:, g * SLAB : (g + 1) * SLAB], v[:, g * SLAB : (g + 1) * SLAB]
            k_dst[g, pl.ds(base, count), :] = kg
            v_dst[g, pl.ds(base, count), :] = vg
            kt_dst[g, :, pl.ds(base, count)] = kg.T
            vt_dst[g, :, pl.ds(base, count)] = vg.T

    def queries(normed, dst, first):
        q = dot(normed, wq_ref[...]).astype(bf16).astype(f32) * HEAD_DIM ** (-0.5)
        for i in range(normed.shape[0] // BLK):
            for g in range(NGRP):
                put_stack(
                    dst,
                    first + i * NGRP + g,
                    q[i * BLK : (i + 1) * BLK, g * SLAB : (g + 1) * SLAB],
                )

    for name in ("x", "wk", "wv", "wq"):
        loads[name].wait()

    def own_rows(r, carry):
        base = pl.multiple_of(r * 256, 256)
        normed, _ = norm_parts(x_ref[pl.ds(base, 256), :].astype(f32))
        normed = (normed * ag_ref[...]).astype(bf16)
        keys_values(normed, base, kown, vown, ktown, vtown)
        queries(normed, qm, r * 2 * NGRP)
        return carry

    lax.fori_loop(0, 2, own_rows, 0, unroll=True)

    loads["nm"].wait()
    for i in range(OWN + 2 * SPAN):
        e = i if i < OWN else (i - OWN - SPAN if i < OWN + SPAN else i - SPAN)
        block = jnp.clip(place * OWN + e, 0, total * OWN - 1)
        line = jnp.where(nm_ref[pl.ds(block, 1), :] > 0, 0.0, FAR).astype(f32)
        live[i * BLK : (i + 1) * BLK, :] = jnp.broadcast_to(line, (BLK, BLK)).T

    def scores(b, g, blocks, keys, first, flags):
        s = dot_last(keys, qm[b * NGRP + g])
        top = jnp.full((1, STK), 4 * FAR, f32)
        for c in range(blocks):
            bias = live[pl.ds(first + c * BLK, BLK), :] + vsc[flags + c]
            part = s[c * BLK : (c + 1) * BLK, :] + lanes4(bias)
            sbuf[g, c * BLK : (c + 1) * BLK, :] = part
            top = jnp.maximum(top, jnp.max(part, axis=0, keepdims=True))
        return top

    def exponentials(b, g, blocks, top, dst):
        count = jnp.zeros((1, STK), f32)
        for c in range(blocks):
            e = jnp.exp(sbuf[g, c * BLK : (c + 1) * BLK, :] - top)
            count = count + jnp.sum(e, axis=0, keepdims=True)
            dst[b * NGRP + g, c * BLK : (c + 1) * BLK, :] = e.astype(bf16)
        return count

    def per_head(slab, row):
        return jnp.concatenate(
            [
                slab[h * HEAD_DIM : (h + 1) * HEAD_DIM, :] * row[:, h * BLK : (h + 1) * BLK]
                for h in range(GRP)
            ],
            axis=0,
        )

    def forward_own(b, carry):
        tops = [scores(b, g, OWN, kown[g], 0, b * OWN) for g in range(NGRP)]
        counts = [exponentials(b, g, OWN, tops[g], eown) for g in range(NGRP)]
        for g in range(NGRP):
            it = b * NGRP + g
            attt[it] = diagonal(dot(vtown[g], eown[it]))
            top_one[pl.ds(it, 1), :] = tops[g]
            count_one[pl.ds(it, 1), :] = counts[g]
        return carry

    lax.fori_loop(0, OWN, forward_own, 0, unroll=True)

    loads["wu"].wait()
    loads["wd"].wait()
    rows.wait_send()
    ring_up = copy(4, wbuf.at[0, member], wbuf.at[1, member], up)
    ring_down = copy(5, wbuf.at[0, member], wbuf.at[2, member], down)
    ring_up.start()
    ring_down.start()
    rows.wait_recv()

    def halo_rows(r, carry):
        side = r // 2
        base = pl.multiple_of(lax.rem(r, 2) * 256, 256)
        normed, _ = norm_parts(halo[side, pl.ds(base, 256), :].astype(f32))
        normed = (normed * ag_ref[...]).astype(bf16)
        n1h[side, pl.ds(base, 256), :] = normed
        keys_values(normed, side * SPAN * BLK + base, khal, vhal, kthal, vthal)
        return carry

    lax.fori_loop(0, 4, halo_rows, 0, unroll=True)

    def window(ref, b, g):
        return ref[g, pl.ds(pl.multiple_of(b * BLK, BLK), HWIN * BLK), :]

    def window_t(ref, b, g):
        return ref[g, :, pl.ds(pl.multiple_of(b * BLK, BLK), HWIN * BLK)]

    def forward_halo(b, carry):
        first = pl.multiple_of(b * BLK, BLK) + OWN * BLK
        tops = [
            scores(b, g, HWIN, window(khal, b, g), first, OWN * OWN + b * HWIN)
            for g in range(NGRP)
        ]
        counts = [exponentials(b, g, HWIN, tops[g], ehal) for g in range(NGRP)]
        for g in range(NGRP):
            it = b * NGRP + g
            far = diagonal(dot(window_t(vthal, b, g), ehal[it]))
            near_top = top_one[pl.ds(it, 1), :]
            top = jnp.maximum(near_top, tops[g])
            near = jnp.exp(near_top - top)
            distant = jnp.exp(tops[g] - top)
            count = count_one[pl.ds(it, 1), :] * near + counts[g] * distant
            inverse = 1.0 / count
            near = near * inverse
            distant = distant * inverse
            mixed = per_head(attt[it], near) + per_head(far, distant)
            attt[it] = mixed
            att[g, pl.ds(pl.multiple_of(b * BLK, BLK), BLK), :] = mixed.T.astype(bf16)
            lse[pl.ds(it, 1), :] = top + jnp.log(count)
            inv_own[pl.ds(it, 1), :] = near
            inv_hal[pl.ds(it, 1), :] = distant
        return carry

    lax.fori_loop(0, OWN, forward_halo, 0, unroll=True)

    levels = Pair(11, lse, lse, lser)
    levels.start()

    loads["wo"].wait()

    def middle(r, carry):
        part = pl.ds(pl.multiple_of(r * 256, 256), 256)
        value = x_ref[part, :].astype(f32) + (
            dot(att[0, part, :], wo_ref[0:SLAB, :]) + dot(att[1, part, :], wo_ref[SLAB:, :])
        )
        mid[part, :] = value
        normed, _ = norm_parts(value)
        n2[part, :] = (normed * fg_ref[...]).astype(bf16)
        acc[part, :] = jnp.zeros((256, acc.shape[1]), f32)
        return carry

    lax.fori_loop(0, 2, middle, 0, unroll=True)
    loads["og"].wait()

    def hidden(slot):
        def run(r, carry):
            part = pl.ds(pl.multiple_of(r * 256, 256), 256)
            pre = dot(n2[part, :], wbuf[slot, 0])
            slope = gelu_slope(pre)
            grad = dot_last(og_ref[part, :], wbuf[slot, 1])
            act = (grad * slope).astype(bf16)
            acc[part, :] += dot_last(act, wbuf[slot, 0])
            return carry

        lax.fori_loop(0, 2, run, 0, unroll=True)

    other = 1 - member

    def arrival(slot_id, slot):
        return copy(slot_id, wbuf.at[slot, other], wbuf.at[slot, other], twin)

    ring_up.wait_recv()
    ring_down.wait_recv()
    cross_up = copy(
        6, wbuf.at[1, member, pl.ds(0, 256)], wbuf.at[3, member, pl.ds(0, 256)], up
    )
    cross_down = copy(
        7, wbuf.at[2, member, pl.ds(256, 256)], wbuf.at[3, member, pl.ds(256, 256)], down
    )
    cross_up.start()
    cross_down.start()
    twin_one = copy(8, wbuf.at[1, member], wbuf.at[1, member], twin)
    twin_two = copy(9, wbuf.at[2, member], wbuf.at[2, member], twin)
    twin_one.start()
    twin_two.start()

    hidden(0)

    def far_queries(r, carry):
        side = r // 2
        base = pl.multiple_of(lax.rem(r, 2) * 256, 256)
        queries(n1h[side, pl.ds(base, 256), :], qmr, r * 2 * NGRP)
        return carry

    lax.fori_loop(0, 4, far_queries, 0, unroll=True)
    arrival(8, 1).wait_recv()
    hidden(1)
    arrival(9, 2).wait_recv()
    hidden(2)

    pairs = []
    for side in range(2):
        begin = 0
        for b in range(OWN):
            first, last = (0, b + 1) if side == 0 else (b, OWN)
            pairs.append((side, b, first, last, begin * BLK))
            begin += last - first

    lists.wait_recv()
    levels.wait_recv()
    for side, b, first, last, begin in pairs:

        def remote_probs(g, carry, side=side, b=b, first=first, last=last, begin=begin):
            it = b * NGRP + g
            level = lser[side, pl.ds(it, 1), :]
            s = dot_last(kown[g, first * BLK : last * BLK, :], qmr[side * NIT + it])
            for c in range(first, last):
                at = (c - first) * BLK
                row = b * OWN + c
                shift = lanes4(vbr[side, row : row + 1, :]) - level
                bias = lanes4(live[c * BLK : (c + 1) * BLK, :]) + shift
                prem[side, g, begin + at : begin + at + BLK, :] = jnp.exp(
                    s[at : at + BLK, :] + bias
                ).astype(bf16)
            return carry

        lax.fori_loop(0, NGRP, remote_probs, 0, unroll=True)

    cross_up.wait_recv()
    cross_down.wait_recv()
    twin_three = copy(10, wbuf.at[3, member], wbuf.at[3, member], twin)
    twin_three.start()
    arrival(10, 3).wait_recv()
    hidden(3)

    for r in range(2):
        part = slice(r * 256, (r + 1) * 256)
        up_grad = og_ref[part, :].astype(f32)
        normed, inverse = norm_parts(mid[part, :])
        res = up_grad + norm_reverse(acc[part, :], normed, inverse, fg_ref[...])
        gmr[part, :] = res
        res_bf = res.astype(bf16)
        n2[part, :] = res_bf
        dob[part, :] = dot_last(res_bf, wo_ref[...]).astype(bf16)

    grads = Pair(13, dob, dob, dor)
    grads.start()

    for r in range(2):
        part = slice(r * 256, (r + 1) * 256)
        grad_wide = dob[part, :].astype(f32)
        grad_t = dot_last(wo_ref[...], n2[part, :]).astype(bf16).astype(f32)
        for i in range(2):
            for g in range(NGRP):
                it = (r * 2 + i) * NGRP + g
                cols = slice(g * SLAB, (g + 1) * SLAB)
                here = slice(i * BLK, (i + 1) * BLK)
                put_stack(dom, it, grad_wide[here, cols])
                product = grad_t[cols, here] * attt[it]
                centre[it : it + 1, :] = jnp.concatenate(
                    [
                        jnp.sum(
                            product[h * HEAD_DIM : (h + 1) * HEAD_DIM], axis=0, keepdims=True
                        )
                        for h in range(GRP)
                    ],
                    axis=1,
                )

    middles = Pair(15, centre, centre, centrer)
    middles.start()

    dk[...] = jnp.zeros(dk.shape, f32)
    dv[...] = jnp.zeros(dv.shape, f32)

    def backward(b, carry):
        for g in range(NGRP):
            it = b * NGRP + g
            grad_stack = dom[it]
            middle_row = centre[pl.ds(it, 1), :]
            grad_prob = dot_last(vown[g], grad_stack)
            probs = eown[it].astype(f32) * inv_own[pl.ds(it, 1), :]
            grad_score = (probs * (grad_prob - middle_row)).astype(bf16)
            dk[g] += dot(grad_score, qm[it])
            dv[g] += dot(probs.astype(bf16), grad_stack)
            wide = dot(ktown[g], grad_score)
            grad_prob = dot_last(window(vhal, b, g), grad_stack)
            probs = ehal[it].astype(f32) * inv_hal[pl.ds(it, 1), :]
            grad_score = (probs * (grad_prob - middle_row)).astype(bf16)
            wide = wide + dot(window_t(kthal, b, g), grad_score)
            dq[g, pl.ds(pl.multiple_of(b * BLK, BLK), BLK), :] = (
                (diagonal(wide) * HEAD_DIM ** (-0.5)).T.astype(bf16)
            )
        return carry

    lax.fori_loop(0, OWN, backward, 0, unroll=True)

    grads.wait_recv()

    for side in range(2):
        for b in range(OWN):
            for g in range(NGRP):
                put_stack(
                    domr,
                    (side * OWN + b) * NGRP + g,
                    dor[side, b * BLK : (b + 1) * BLK, g * SLAB : (g + 1) * SLAB].astype(f32),
                )
    middles.wait_recv()

    for side, b, first, last, begin in pairs:

        def remote(g, carry, side=side, b=b, first=first, last=last, begin=begin):
            it = b * NGRP + g
            grad_stack = domr[side * NIT + it]
            own = slice(first * BLK, last * BLK)
            probs = prem[side, g, begin : begin + (last - first) * BLK, :]
            grad_prob = dot_last(vown[g, own, :], grad_stack)
            grad_score = probs.astype(f32) * (grad_prob - centrer[side, pl.ds(it, 1), :])
            dk[g, own, :] += dot(grad_score.astype(bf16), qmr[side * NIT + it])
            dv[g, own, :] += dot(probs, grad_stack)
            return carry

        lax.fori_loop(0, NGRP, remote, 0, unroll=True)

    def finish(r, carry):
        part = pl.ds(pl.multiple_of(r * 256, 256), 256)
        grad = None
        for g in range(NGRP):
            cols = slice(g * SLAB, (g + 1) * SLAB)
            term = dot_last(dq[g, part, :], wq_ref[:, cols])
            term += dot_last(dk[g, part, :].astype(bf16), wk_ref[:, cols])
            term += dot_last(dv[g, part, :].astype(bf16), wv_ref[:, cols])
            grad = term if grad is None else grad + term
        normed, inverse = norm_parts(x_ref[part, :].astype(f32))
        out_ref[part, :] = (
            gmr[part, :] + norm_reverse(grad, normed, inverse, ag_ref[...])
        ).astype(out_ref.dtype)
        return carry

    lax.fori_loop(0, 2, finish, 0, unroll=True)

    for done in (
        lists,
        levels,
        middles,
        grads,
        ring_up,
        ring_down,
        cross_up,
        cross_down,
        twin_one,
        twin_two,
        twin_three,
    ):
        done.wait_send()


def body(nodes, tensors, *args):
    (x, og, ag, fg, wq, wk, wv, wo, wu, wd, nbr, cnt, nm) = args
    rows, width = x.shape
    vm = pl.BlockSpec(memory_space=pltpu.VMEM)
    sm = pl.BlockSpec(memory_space=pltpu.SMEM)
    hbm = pl.BlockSpec(memory_space=pl.ANY)
    V = pltpu.VMEM
    own, hal = OWN * BLK, 2 * SPAN * BLK
    return pl.pallas_call(
        functools.partial(kernel, nodes, tensors),
        out_shape=jax.ShapeDtypeStruct((rows, width), bf16),
        in_specs=[hbm] * 2 + [vm] * 2 + [hbm] * 6 + [sm] * 2 + [hbm],
        out_specs=vm,
        scratch_shapes=[
            V((rows, width), bf16),
            V((rows, width), bf16),
            V((width, width), bf16),
            V((width, width), bf16),
            V((width, width), bf16),
            V((width, width), bf16),
            V(nm.shape, jnp.int32),
            V((2, rows, width), bf16),
            V((2, rows, width), bf16),
            V((NIT, STK, SLAB), bf16),
            V((2 * NIT, STK, SLAB), bf16),
            V((NGRP, own, SLAB), bf16),
            V((NGRP, own, SLAB), bf16),
            V((NGRP, SLAB, own), bf16),
            V((NGRP, SLAB, own), bf16),
            V((NGRP, hal, SLAB), bf16),
            V((NGRP, hal, SLAB), bf16),
            V((NGRP, SLAB, hal), bf16),
            V((NGRP, SLAB, hal), bf16),
            V((own + hal, BLK), f32),
            pltpu.SMEM((OWN * (OWN + HWIN),), f32),
            V((2, OWN * OWN, BLK), f32),
            V((2, OWN * OWN, BLK), f32),
            V((4, 2, width, width), bf16),
            V((NGRP, HWIN * BLK, STK), f32),
            V((NIT, own, STK), bf16),
            V((NIT, HWIN * BLK, STK), bf16),
            V((NGRP, rows, SLAB), bf16),
            V((NIT, SLAB, BLK), f32),
            V((NIT, STK), f32),
            V((NIT, STK), f32),
            V((NIT, STK), f32),
            V((2, NIT, STK), f32),
            V((NIT, STK), f32),
            V((2, NIT, STK), f32),
            V((NIT, STK), f32),
            V((NIT, STK), f32),
            V((rows, width), f32),
            V((rows, width), bf16),
            V((rows, width), f32),
            V((rows, width), f32),
            V((rows, width), bf16),
            V((2, rows, width), bf16),
            V((NIT, STK, SLAB), bf16),
            V((2 * NIT, STK, SLAB), bf16),
            V((2, NGRP, OWN * (OWN + 1) // 2 * BLK, STK), bf16),
            V((NGRP, rows, SLAB), bf16),
            V((NGRP, rows, SLAB), f32),
            V((NGRP, rows, SLAB), f32),
            pltpu.SemaphoreType.DMA((17,)),
            pltpu.SemaphoreType.DMA((17,)),
            pltpu.SemaphoreType.DMA((9,)),
        ],
        compiler_params=pltpu.CompilerParams(
            collective_id=0, has_side_effects=True, vmem_limit_bytes=62 * 1024 * 1024
        ),
    )(x, og, ag.reshape(1, width), fg.reshape(1, width), wq, wk, wv, wo, wu, wd, nbr, cnt, nm)


def solution(mesh):
    return jax.shard_map(
        functools.partial(body, mesh.shape["node"], mesh.shape["tensor"]),
        mesh=mesh,
        in_specs=(
            P(("member", "node", "tensor"), None),
            P(("member", "node", "tensor"), None),
            P(),
            P(),
            P(),
            P(),
            P(),
            P(),
            P(None, "tensor"),
            P("tensor", None),
            P(("node", "tensor"), None),
            P(("node", "tensor")),
            P(),
        ),
        out_specs=P(("member", "node", "tensor"), None),
        check_vma=False,
    )
```

```python
import functools

import jax
import jax.numpy as jnp
from jax import lax
from jax.experimental import pallas as pl
from jax.experimental.pallas import tpu as pltpu
from jax.sharding import PartitionSpec as P

HEADS = 8
HEAD_DIM = 64
NBR = 8
SPAN = 4
BLK = 128
OWN = 4
HWIN = SPAN + 1
GRP = 4
SLAB = GRP * HEAD_DIM
NGRP = HEADS // GRP
STK = GRP * BLK
NIT = OWN * NGRP
RING = 4
QUART = 128

NORM_EPS = 1e-05
GELU_C = 0.7978845608028654
GELU_A = 0.044715
FAR = -1e30

f32 = jnp.float32
bf16 = jnp.bfloat16
MESH = pl.DeviceIdType.MESH


def dot(left, right):
    return jnp.dot(left, right, preferred_element_type=f32)


def dot_last(left, right):
    return lax.dot_general(left, right, (((1,), (1,)), ((), ())), preferred_element_type=f32)


def norm_parts(values):
    centre = jnp.mean(values, axis=-1, keepdims=True)
    centred = values - centre
    inverse = lax.rsqrt(jnp.mean(centred * centred, axis=-1, keepdims=True) + NORM_EPS)
    return centred * inverse, inverse


def norm_reverse(upstream, normed, inverse, gain):
    scaled = upstream * gain
    first = jnp.mean(scaled, axis=-1, keepdims=True)
    second = jnp.mean(scaled * normed, axis=-1, keepdims=True)
    return inverse * (scaled - first - normed * second)


def gelu_slope(v):
    square = v * v
    tangent = jnp.tanh(v * (GELU_C + GELU_C * GELU_A * square))
    return 0.5 * (1.0 + tangent) + (0.5 * v) * (1.0 - tangent * tangent) * (
        GELU_C + 3.0 * GELU_C * GELU_A * square
    )


def lanes4(tile):
    return jnp.concatenate([tile] * GRP, axis=1)


def put_stack(dst, index, slab):
    head = lax.broadcasted_iota(jnp.int32, (BLK, SLAB), 1) // HEAD_DIM
    for h in range(GRP):
        dst[index, h * BLK : (h + 1) * BLK, :] = jnp.where(head == h, slab, 0.0).astype(bf16)


def diagonal(wide):
    return jnp.concatenate(
        [
            wide[h * HEAD_DIM : (h + 1) * HEAD_DIM, h * BLK : (h + 1) * BLK]
            for h in range(GRP)
        ],
        axis=0,
    )


def kernel(
    nodes,
    tensors,
    x_hbm,
    og_hbm,
    ag_ref,
    fg_ref,
    wq_hbm,
    wk_hbm,
    wv_hbm,
    wo_hbm,
    wu_hbm,
    wd_hbm,
    nbr_ref,
    cnt_ref,
    nm_hbm,
    out_ref,
    x_ref,
    og_ref,
    wq_ref,
    wk_ref,
    wv_ref,
    wo_ref,
    nm_ref,
    halo,
    n1h,
    qm,
    qmr,
    kown,
    vown,
    ktown,
    vtown,
    khal,
    vhal,
    kthal,
    vthal,
    live,
    vsc,
    vbs,
    vbr,
    wbuf,
    sbuf,
    eown,
    ehal,
    att,
    attt,
    top_one,
    count_one,
    lse,
    lser,
    centre,
    centrer,
    inv_own,
    inv_hal,
    mid,
    n2,
    acc,
    gmr,
    dob,
    dor,
    dom,
    domr,
    prem,
    dq,
    dk,
    dv,
    send,
    recv,
    local,
):
    member = lax.axis_index("member")
    node = lax.axis_index("node")
    tensor = lax.axis_index("tensor")
    total = nodes * tensors
    place = node * tensors + tensor
    has_left = place > 0
    has_right = place < total - 1
    after = lax.rem(place + 1, total)
    before = lax.rem(place + total - 1, total)
    right = (member, after // tensors, lax.rem(after, tensors))
    left = (member, before // tensors, lax.rem(before, tensors))
    up = (member, node, lax.rem(tensor + 1, tensors))
    down = (member, node, lax.rem(tensor + tensors - 1, tensors))
    twin = (1 - member, node, tensor)
    column = lax.rem(node, RING)
    plane = node - column
    east = (member, plane + lax.rem(column + 1, RING), tensor)
    west = (member, plane + lax.rem(column + RING - 1, RING), tensor)

    loads = {}
    for i, (name, src, dst) in enumerate(
        (
            ("wu", wu_hbm, wbuf.at[0, 0]),
            ("wd", wd_hbm, wbuf.at[0, 1]),
            ("x", x_hbm, x_ref),
            ("wk", wk_hbm, wk_ref),
            ("wv", wv_hbm, wv_ref),
            ("wq", wq_hbm, wq_ref),
            ("nm", nm_hbm, nm_ref),
            ("wo", wo_hbm, wo_ref),
            ("og", og_hbm, og_ref),
        )
    ):
        loads[name] = pltpu.make_async_copy(src, dst, local.at[i])
        loads[name].start()

    barrier = pltpu.get_barrier_semaphore()
    for peer in (up, down, east, west, twin):
        pl.semaphore_signal(barrier, inc=1, device_id=peer, device_id_type=MESH)

    @pl.when(has_right)
    def _():
        pl.semaphore_signal(barrier, inc=1, device_id=right, device_id_type=MESH)

    @pl.when(has_left)
    def _():
        pl.semaphore_signal(barrier, inc=1, device_id=left, device_id_type=MESH)

    pl.semaphore_wait(barrier, 5 + has_right.astype(jnp.int32) + has_left.astype(jnp.int32))

    def copy(slot, src, dst, peer):
        return pltpu.make_async_remote_copy(
            src_ref=src,
            dst_ref=dst,
            send_sem=send.at[slot],
            recv_sem=recv.at[slot],
            device_id=peer,
            device_id_type=MESH,
        )

    class Pair:
        def __init__(self, slot, to_right, to_left, dst):
            self.to_right = lambda: copy(slot, to_right, dst.at[0], right)
            self.to_left = lambda: copy(slot + 1, to_left, dst.at[1], left)

        def each(self, right_one, left_one, do):
            @pl.when(right_one)
            def _():
                do(self.to_right())

            @pl.when(left_one)
            def _():
                do(self.to_left())

        def start(self):
            self.each(has_right, has_left, lambda c: c.start())

        def wait_send(self):
            self.each(has_right, has_left, lambda c: c.wait_send())

        def wait_recv(self):
            self.each(has_left, has_right, lambda c: c.wait_recv())

    def quarter(turn, start=0, count=QUART):
        place_x = lax.rem(column + turn + RING, RING)
        return pl.ds(pl.multiple_of(place_x * QUART + start, 64), count)

    def stripe(first, parts, chunk):
        return wbuf.at[pl.ds(first, parts), member, chunk]

    mine = quarter(0)

    class Pull:
        def __init__(self, slot, part, peer):
            self.made = lambda src: copy(slot, src.at[mine], wbuf.at[part, member, mine], peer)

        def start(self):
            @pl.when(member == 0)
            def _():
                self.made(wu_hbm).start()

            @pl.when(member == 1)
            def _():
                self.made(wd_hbm).start()

        def wait_send(self):
            self.made(wu_hbm).wait_send()

        def wait_recv(self):
            self.made(wu_hbm).wait_recv()

    pull_up = Pull(4, 1, up)
    pull_down = Pull(5, 2, down)
    pull_up.start()
    pull_down.start()

    class Halves:
        def __init__(self, slots, src, dst):
            self.parts = [
                Pair(slot, src.at[half], src.at[half], dst.at[:, half])
                for slot, half in zip(slots, (pl.ds(0, 256), pl.ds(256, 256)))
            ]

        def wait_send(self):
            for part in self.parts:
                part.wait_send()

    rows = Halves((0, 24), x_hbm, halo)
    rows.parts[0].start()
    rows.parts[1].start()

    def listed(b, wanted):
        hit = jnp.int32(0)
        for j in range(NBR):
            same = (nbr_ref[b, j] == wanted) & (j < cnt_ref[b])
            hit = hit | same.astype(jnp.int32)
        return jnp.where(hit > 0, 0.0, FAR).astype(f32)

    def valid_row(b, carry):
        for c in range(OWN):
            vsc[b * OWN + c] = listed(b, place * OWN + c)
        for j in range(HWIN):
            e = b + j
            vsc[OWN * OWN + b * HWIN + j] = listed(
                b, place * OWN + jnp.where(e < SPAN, e - SPAN, e - SPAN + OWN)
            )
        return carry

    lax.fori_loop(0, OWN, valid_row, 0)
    for b in range(OWN):
        for e in range(OWN):
            row = b * OWN + e
            base = OWN * OWN + b * HWIN
            low = vsc[base + e - b] if e >= b else jnp.float32(FAR)
            high = vsc[base + SPAN + e - b] if e <= b else jnp.float32(FAR)
            vbs[0, row : row + 1, :] = jnp.full((1, BLK), low, f32)
            vbs[1, row : row + 1, :] = jnp.full((1, BLK), high, f32)
    lists = Pair(2, vbs.at[1], vbs.at[0], vbr)
    lists.start()

    @pl.when(jnp.logical_not(has_left))
    def _():
        vbr[0] = jnp.full(vbr.shape[1:], FAR, f32)
        lser[0] = jnp.zeros(lser.shape[1:], f32)
        centrer[0] = jnp.zeros(centrer.shape[1:], f32)
        halo[0] = jnp.zeros(halo.shape[1:], bf16)
        dor[0] = jnp.zeros(dor.shape[1:], bf16)

    @pl.when(jnp.logical_not(has_right))
    def _():
        vbr[1] = jnp.full(vbr.shape[1:], FAR, f32)
        lser[1] = jnp.zeros(lser.shape[1:], f32)
        centrer[1] = jnp.zeros(centrer.shape[1:], f32)
        halo[1] = jnp.zeros(halo.shape[1:], bf16)
        dor[1] = jnp.zeros(dor.shape[1:], bf16)

    def keys_values(normed, base, k_dst, v_dst, kt_dst, vt_dst):
        count = normed.shape[0]
        base = pl.multiple_of(base, BLK)
        k = dot(normed, wk_ref[...]).astype(bf16)
        v = dot(normed, wv_ref[...]).astype(bf16)
        for g in range(NGRP):
            kg, vg = k[:, g * SLAB : (g + 1) * SLAB], v[:, g * SLAB : (g + 1) * SLAB]
            k_dst[g, pl.ds(base, count), :] = kg
            v_dst[g, pl.ds(base, count), :] = vg
            kt_dst[g, :, pl.ds(base, count)] = kg.T
            vt_dst[g, :, pl.ds(base, count)] = vg.T

    def queries(normed, dst, first):
        q = dot(normed, wq_ref[...]).astype(bf16).astype(f32) * HEAD_DIM ** (-0.5)
        for i in range(normed.shape[0] // BLK):
            for g in range(NGRP):
                put_stack(
                    dst,
                    first + i * NGRP + g,
                    q[i * BLK : (i + 1) * BLK, g * SLAB : (g + 1) * SLAB],
                )

    for name in ("x", "wk", "wv", "wq"):
        loads[name].wait()

    def own_rows(r, carry):
        base = pl.multiple_of(r * 256, 256)
        normed, _ = norm_parts(x_ref[pl.ds(base, 256), :].astype(f32))
        normed = (normed * ag_ref[...]).astype(bf16)
        keys_values(normed, base, kown, vown, ktown, vtown)
        queries(normed, qm, r * 2 * NGRP)
        return carry

    lax.fori_loop(0, 2, own_rows, 0, unroll=True)

    loads["nm"].wait()
    for i in range(OWN + 2 * SPAN):
        e = i if i < OWN else (i - OWN - SPAN if i < OWN + SPAN else i - SPAN)
        block = jnp.clip(place * OWN + e, 0, total * OWN - 1)
        line = jnp.where(nm_ref[pl.ds(block, 1), :] > 0, 0.0, FAR).astype(f32)
        live[i * BLK : (i + 1) * BLK, :] = jnp.broadcast_to(line, (BLK, BLK)).T

    def scores(b, g, blocks, keys, first, flags):
        s = dot_last(keys, qm[b * NGRP + g])
        top = jnp.full((1, STK), 4 * FAR, f32)
        for c in range(blocks):
            bias = live[pl.ds(first + c * BLK, BLK), :] + vsc[flags + c]
            part = s[c * BLK : (c + 1) * BLK, :] + lanes4(bias)
            sbuf[g, c * BLK : (c + 1) * BLK, :] = part
            top = jnp.maximum(top, jnp.max(part, axis=0, keepdims=True))
        return top

    def exponentials(b, g, blocks, top, dst):
        count = jnp.zeros((1, STK), f32)
        for c in range(blocks):
            e = jnp.exp(sbuf[g, c * BLK : (c + 1) * BLK, :] - top)
            count = count + jnp.sum(e, axis=0, keepdims=True)
            dst[b * NGRP + g, c * BLK : (c + 1) * BLK, :] = e.astype(bf16)
        return count

    def per_head(slab, row):
        return jnp.concatenate(
            [
                slab[h * HEAD_DIM : (h + 1) * HEAD_DIM, :] * row[:, h * BLK : (h + 1) * BLK]
                for h in range(GRP)
            ],
            axis=0,
        )

    def forward_own(b, carry):
        tops = [scores(b, g, OWN, kown[g], 0, b * OWN) for g in range(NGRP)]
        counts = [exponentials(b, g, OWN, tops[g], eown) for g in range(NGRP)]
        for g in range(NGRP):
            it = b * NGRP + g
            attt[it] = diagonal(dot(vtown[g], eown[it]))
            top_one[pl.ds(it, 1), :] = tops[g]
            count_one[pl.ds(it, 1), :] = counts[g]
        return carry

    lax.fori_loop(0, OWN, forward_own, 0, unroll=True)

    def hand_over(slot, first, parts, chunk):
        made = copy(slot, stripe(first, parts, chunk), stripe(first, parts, chunk), twin)
        made.start()
        handed.append((made, slot, first, parts, chunk))

    handed = []

    pull_up.wait_recv()
    pull_down.wait_recv()
    half_low, half_high = quarter(0, 0, 64), quarter(0, 64, 64)
    cross_up = copy(6, wbuf.at[1, member, half_low], wbuf.at[3, member, half_low], up)
    cross_down = copy(7, wbuf.at[2, member, half_high], wbuf.at[3, member, half_high], down)
    cross_up.start()
    cross_down.start()
    near_east = copy(8, stripe(1, 2, mine), stripe(1, 2, mine), east)
    near_west = copy(9, stripe(1, 2, mine), stripe(1, 2, mine), west)
    near_east.start()
    near_west.start()
    hand_over(20, 1, 2, mine)

    cross_up.wait_recv()
    cross_down.wait_recv()
    far_east = copy(10, stripe(3, 1, mine), stripe(3, 1, mine), east)
    far_west = copy(17, stripe(3, 1, mine), stripe(3, 1, mine), west)
    far_east.start()
    far_west.start()

    near_east.wait_recv()
    near_west.wait_recv()
    from_west, from_east = quarter(-1, 0, 64), quarter(1, 64, 64)
    on_east = copy(18, stripe(1, 2, from_west), stripe(1, 2, from_west), east)
    on_west = copy(19, stripe(1, 2, from_east), stripe(1, 2, from_east), west)
    on_east.start()
    on_west.start()
    hand_over(23, 1, 2, quarter(-1))
    hand_over(26, 1, 2, quarter(1))

    def halo_rows(r, carry):
        side = lax.rem(r, 2)
        base = pl.multiple_of((r // 2) * 256, 256)
        normed, _ = norm_parts(halo[side, pl.ds(base, 256), :].astype(f32))
        normed = (normed * ag_ref[...]).astype(bf16)
        n1h[side, pl.ds(base, 256), :] = normed
        keys_values(normed, side * SPAN * BLK + base, khal, vhal, kthal, vthal)
        return carry

    for half in range(2):
        rows.parts[half].wait_recv()
        lax.fori_loop(2 * half, 2 * half + 2, halo_rows, 0, unroll=True)

    def window(ref, b, g):
        return ref[g, pl.ds(pl.multiple_of(b * BLK, BLK), HWIN * BLK), :]

    def window_t(ref, b, g):
        return ref[g, :, pl.ds(pl.multiple_of(b * BLK, BLK), HWIN * BLK)]

    def forward_halo(b, carry):
        first = pl.multiple_of(b * BLK, BLK) + OWN * BLK
        tops = [
            scores(b, g, HWIN, window(khal, b, g), first, OWN * OWN + b * HWIN)
            for g in range(NGRP)
        ]
        counts = [exponentials(b, g, HWIN, tops[g], ehal) for g in range(NGRP)]
        for g in range(NGRP):
            it = b * NGRP + g
            far = diagonal(dot(window_t(vthal, b, g), ehal[it]))
            near_top = top_one[pl.ds(it, 1), :]
            top = jnp.maximum(near_top, tops[g])
            near = jnp.exp(near_top - top)
            distant = jnp.exp(tops[g] - top)
            count = count_one[pl.ds(it, 1), :] * near + counts[g] * distant
            inverse = 1.0 / count
            near = near * inverse
            distant = distant * inverse
            mixed = per_head(attt[it], near) + per_head(far, distant)
            attt[it] = mixed
            att[g, pl.ds(pl.multiple_of(b * BLK, BLK), BLK), :] = mixed.T.astype(bf16)
            lse[pl.ds(it, 1), :] = top + jnp.log(count)
            inv_own[pl.ds(it, 1), :] = near
            inv_hal[pl.ds(it, 1), :] = distant
        return carry

    lax.fori_loop(0, 2, forward_halo, 0, unroll=True)

    far_east.wait_recv()
    far_west.wait_recv()
    last_east = copy(21, stripe(3, 1, from_west), stripe(3, 1, from_west), east)
    last_west = copy(22, stripe(3, 1, from_east), stripe(3, 1, from_east), west)
    last_east.start()
    last_west.start()
    on_east.wait_recv()
    on_west.wait_recv()
    hand_over(27, 1, 2, quarter(2))
    hand_over(28, 3, 1, mine)
    hand_over(29, 3, 1, quarter(-1))
    hand_over(30, 3, 1, quarter(1))

    lax.fori_loop(2, OWN, forward_halo, 0, unroll=True)

    levels = Pair(11, lse, lse, lser)
    levels.start()

    loads["wo"].wait()

    def middle(r, carry):
        part = pl.ds(pl.multiple_of(r * 256, 256), 256)
        value = x_ref[part, :].astype(f32) + (
            dot(att[0, part, :], wo_ref[0:SLAB, :]) + dot(att[1, part, :], wo_ref[SLAB:, :])
        )
        mid[part, :] = value
        normed, _ = norm_parts(value)
        n2[part, :] = (normed * fg_ref[...]).astype(bf16)
        acc[part, :] = jnp.zeros((256, acc.shape[1]), f32)
        return carry

    lax.fori_loop(0, 2, middle, 0, unroll=True)
    loads["og"].wait()
    loads["wu"].wait()
    loads["wd"].wait()

    def hidden(slot):
        def run(r, carry):
            part = pl.ds(pl.multiple_of(r * 256, 256), 256)
            pre = dot(n2[part, :], wbuf[slot, 0])
            slope = gelu_slope(pre)
            grad = dot_last(og_ref[part, :], wbuf[slot, 1])
            act = (grad * slope).astype(bf16)
            acc[part, :] += dot_last(act, wbuf[slot, 0])
            return carry

        lax.fori_loop(0, 2, run, 0, unroll=True)

    other = 1 - member

    def handed_here(first):
        for _, slot, begin, parts, chunk in handed:
            if begin == first:
                landed = wbuf.at[pl.ds(begin, parts), other, chunk]
                copy(slot, landed, landed, twin).wait_recv()

    hidden(0)
    last_east.wait_recv()
    last_west.wait_recv()
    hand_over(31, 3, 1, quarter(2))
    handed_here(1)
    hidden(1)
    hidden(2)
    handed_here(3)
    hidden(3)

    grads = Halves((13, 32), dob, dor)
    for r in range(2):
        part = slice(r * 256, (r + 1) * 256)
        up_grad = og_ref[part, :].astype(f32)
        normed, inverse = norm_parts(mid[part, :])
        res = up_grad + norm_reverse(acc[part, :], normed, inverse, fg_ref[...])
        gmr[part, :] = res
        res_bf = res.astype(bf16)
        n2[part, :] = res_bf
        dob[part, :] = dot_last(res_bf, wo_ref[...]).astype(bf16)
        grads.parts[r].start()

    for r in range(2):
        part = slice(r * 256, (r + 1) * 256)
        grad_wide = dob[part, :].astype(f32)
        grad_t = dot_last(wo_ref[...], n2[part, :]).astype(bf16).astype(f32)
        for i in range(2):
            for g in range(NGRP):
                it = (r * 2 + i) * NGRP + g
                cols = slice(g * SLAB, (g + 1) * SLAB)
                here = slice(i * BLK, (i + 1) * BLK)
                put_stack(dom, it, grad_wide[here, cols])
                product = grad_t[cols, here] * attt[it]
                centre[it : it + 1, :] = jnp.concatenate(
                    [
                        jnp.sum(
                            product[h * HEAD_DIM : (h + 1) * HEAD_DIM], axis=0, keepdims=True
                        )
                        for h in range(GRP)
                    ],
                    axis=1,
                )

    middles = Pair(15, centre, centre, centrer)
    middles.start()

    dk[...] = jnp.zeros(dk.shape, f32)
    dv[...] = jnp.zeros(dv.shape, f32)

    def backward(b, carry):
        for g in range(NGRP):
            it = b * NGRP + g
            grad_stack = dom[it]
            middle_row = centre[pl.ds(it, 1), :]
            grad_prob = dot_last(vown[g], grad_stack)
            probs = eown[it].astype(f32) * inv_own[pl.ds(it, 1), :]
            grad_score = (probs * (grad_prob - middle_row)).astype(bf16)
            dk[g] += dot(grad_score, qm[it])
            dv[g] += dot(probs.astype(bf16), grad_stack)
            wide = dot(ktown[g], grad_score)
            grad_prob = dot_last(window(vhal, b, g), grad_stack)
            probs = ehal[it].astype(f32) * inv_hal[pl.ds(it, 1), :]
            grad_score = (probs * (grad_prob - middle_row)).astype(bf16)
            wide = wide + dot(window_t(kthal, b, g), grad_score)
            dq[g, pl.ds(pl.multiple_of(b * BLK, BLK), BLK), :] = (
                (diagonal(wide) * HEAD_DIM ** (-0.5)).T.astype(bf16)
            )
        return carry

    lax.fori_loop(0, OWN, backward, 0, unroll=True)

    def far_queries(r, carry):
        side = r // 2
        base = pl.multiple_of(lax.rem(r, 2) * 256, 256)
        queries(n1h[side, pl.ds(base, 256), :], qmr, r * 2 * NGRP)
        return carry

    lax.fori_loop(0, 4, far_queries, 0, unroll=True)
    pairs = []
    for side in range(2):
        begin = 0
        for b in range(OWN):
            first, last = (0, b + 1) if side == 0 else (b, OWN)
            pairs.append((side, b, first, last, begin * BLK))
            begin += last - first
    pairs.sort(key=lambda pair: pair[1])

    lists.wait_recv()
    levels.wait_recv()
    for side, b, first, last, begin in pairs:

        def remote_probs(g, carry, side=side, b=b, first=first, last=last, begin=begin):
            it = b * NGRP + g
            level = lser[side, pl.ds(it, 1), :]
            s = dot_last(kown[g, first * BLK : last * BLK, :], qmr[side * NIT + it])
            for c in range(first, last):
                at = (c - first) * BLK
                row = b * OWN + c
                shift = lanes4(vbr[side, row : row + 1, :]) - level
                bias = lanes4(live[c * BLK : (c + 1) * BLK, :]) + shift
                prem[side, g, begin + at : begin + at + BLK, :] = jnp.exp(
                    s[at : at + BLK, :] + bias
                ).astype(bf16)
            return carry

        lax.fori_loop(0, NGRP, remote_probs, 0, unroll=True)

    middles.wait_recv()
    for half in range(2):
        grads.parts[half].wait_recv()
        for side, b, first, last, begin in pairs[half * OWN : (half + 1) * OWN]:
            for g in range(NGRP):
                it = side * NIT + b * NGRP + g
                put_stack(
                    domr,
                    it,
                    dor[side, b * BLK : (b + 1) * BLK, g * SLAB : (g + 1) * SLAB].astype(f32),
                )
                grad_stack = domr[it]
                own = slice(first * BLK, last * BLK)
                probs = prem[side, g, begin : begin + (last - first) * BLK, :]
                grad_prob = dot_last(vown[g, own, :], grad_stack)
                middle_row = centrer[side, b * NGRP + g : b * NGRP + g + 1, :]
                grad_score = (probs.astype(f32) * (grad_prob - middle_row)).astype(bf16)
                dk[g, own, :] += dot(grad_score, qmr[it])
                dv[g, own, :] += dot(probs, grad_stack)

    def finish(r, carry):
        part = pl.ds(pl.multiple_of(r * 256, 256), 256)
        grad = None
        for g in range(NGRP):
            cols = slice(g * SLAB, (g + 1) * SLAB)
            term = dot_last(dq[g, part, :], wq_ref[:, cols])
            term += dot_last(dk[g, part, :].astype(bf16), wk_ref[:, cols])
            term += dot_last(dv[g, part, :].astype(bf16), wv_ref[:, cols])
            grad = term if grad is None else grad + term
        normed, inverse = norm_parts(x_ref[part, :].astype(f32))
        out_ref[part, :] = (
            gmr[part, :] + norm_reverse(grad, normed, inverse, ag_ref[...])
        ).astype(out_ref.dtype)
        return carry

    lax.fori_loop(0, 2, finish, 0, unroll=True)

    for done in (
        rows,
        lists,
        levels,
        middles,
        grads,
        pull_up,
        pull_down,
        cross_up,
        cross_down,
        near_east,
        near_west,
        far_east,
        far_west,
        on_east,
        on_west,
        last_east,
        last_west,
        *[made for made, *_ in handed],
    ):
        done.wait_send()


def body(nodes, tensors, *args):
    (x, og, ag, fg, wq, wk, wv, wo, wu, wd, nbr, cnt, nm) = args
    rows, width = x.shape
    vm = pl.BlockSpec(memory_space=pltpu.VMEM)
    sm = pl.BlockSpec(memory_space=pltpu.SMEM)
    hbm = pl.BlockSpec(memory_space=pl.ANY)
    V = pltpu.VMEM
    own, hal = OWN * BLK, 2 * SPAN * BLK
    return pl.pallas_call(
        functools.partial(kernel, nodes, tensors),
        out_shape=jax.ShapeDtypeStruct((rows, width), bf16),
        in_specs=[hbm] * 2 + [vm] * 2 + [hbm] * 6 + [sm] * 2 + [hbm],
        out_specs=vm,
        scratch_shapes=[
            V((rows, width), bf16),
            V((rows, width), bf16),
            V((width, width), bf16),
            V((width, width), bf16),
            V((width, width), bf16),
            V((width, width), bf16),
            V(nm.shape, jnp.int32),
            V((2, rows, width), bf16),
            V((2, rows, width), bf16),
            V((NIT, STK, SLAB), bf16),
            V((2 * NIT, STK, SLAB), bf16),
            V((NGRP, own, SLAB), bf16),
            V((NGRP, own, SLAB), bf16),
            V((NGRP, SLAB, own), bf16),
            V((NGRP, SLAB, own), bf16),
            V((NGRP, hal, SLAB), bf16),
            V((NGRP, hal, SLAB), bf16),
            V((NGRP, SLAB, hal), bf16),
            V((NGRP, SLAB, hal), bf16),
            V((own + hal, BLK), f32),
            pltpu.SMEM((OWN * (OWN + HWIN),), f32),
            V((2, OWN * OWN, BLK), f32),
            V((2, OWN * OWN, BLK), f32),
            V((4, 2, width, width), bf16),
            V((NGRP, HWIN * BLK, STK), f32),
            V((NIT, own, STK), bf16),
            V((NIT, HWIN * BLK, STK), bf16),
            V((NGRP, rows, SLAB), bf16),
            V((NIT, SLAB, BLK), f32),
            V((NIT, STK), f32),
            V((NIT, STK), f32),
            V((NIT, STK), f32),
            V((2, NIT, STK), f32),
            V((NIT, STK), f32),
            V((2, NIT, STK), f32),
            V((NIT, STK), f32),
            V((NIT, STK), f32),
            V((rows, width), f32),
            V((rows, width), bf16),
            V((rows, width), f32),
            V((rows, width), f32),
            V((rows, width), bf16),
            V((2, rows, width), bf16),
            V((NIT, STK, SLAB), bf16),
            V((2 * NIT, STK, SLAB), bf16),
            V((2, NGRP, OWN * (OWN + 1) // 2 * BLK, STK), bf16),
            V((NGRP, rows, SLAB), bf16),
            V((NGRP, rows, SLAB), f32),
            V((NGRP, rows, SLAB), f32),
            pltpu.SemaphoreType.DMA((34,)),
            pltpu.SemaphoreType.DMA((34,)),
            pltpu.SemaphoreType.DMA((9,)),
        ],
        compiler_params=pltpu.CompilerParams(
            collective_id=0, has_side_effects=True, vmem_limit_bytes=62 * 1024 * 1024
        ),
    )(x, og, ag.reshape(1, width), fg.reshape(1, width), wq, wk, wv, wo, wu, wd, nbr, cnt, nm)


def solution(mesh):
    return jax.shard_map(
        functools.partial(body, mesh.shape["node"], mesh.shape["tensor"]),
        mesh=mesh,
        in_specs=(
            P(("member", "node", "tensor"), None),
            P(("member", "node", "tensor"), None),
            P(),
            P(),
            P(),
            P(),
            P(),
            P(),
            P(None, "tensor"),
            P("tensor", None),
            P(("node", "tensor"), None),
            P(("node", "tensor")),
            P(),
        ),
        out_specs=P(("member", "node", "tensor"), None),
        check_vma=False,
    )
```

```python
import functools

import jax
import jax.numpy as jnp
from jax import lax
from jax.experimental import pallas as pl
from jax.experimental.pallas import tpu as pltpu
from jax.sharding import PartitionSpec as P

HEADS = 8
HEAD_DIM = 64
NBR = 8
SPAN = 4
BLK = 128
OWN = 4
HWIN = SPAN + 1
GRP = 4
SLAB = GRP * HEAD_DIM
NGRP = HEADS // GRP
STK = GRP * BLK
NIT = OWN * NGRP
RING = 4
QUART = 128

NORM_EPS = 1e-05
GELU_C = 0.7978845608028654
GELU_A = 0.044715
FAR = -1e30

f32 = jnp.float32
bf16 = jnp.bfloat16
MESH = pl.DeviceIdType.MESH


def dot(left, right):
    return jnp.dot(left, right, preferred_element_type=f32)


def dot_last(left, right):
    return lax.dot_general(left, right, (((1,), (1,)), ((), ())), preferred_element_type=f32)


def norm_parts(values):
    centre = jnp.mean(values, axis=-1, keepdims=True)
    centred = values - centre
    inverse = lax.rsqrt(jnp.mean(centred * centred, axis=-1, keepdims=True) + NORM_EPS)
    return centred * inverse, inverse


def norm_reverse(upstream, normed, inverse, gain):
    scaled = upstream * gain
    first = jnp.mean(scaled, axis=-1, keepdims=True)
    second = jnp.mean(scaled * normed, axis=-1, keepdims=True)
    return inverse * (scaled - first - normed * second)


def gelu_slope(v):
    square = v * v
    tangent = jnp.tanh(v * (GELU_C + GELU_C * GELU_A * square))
    return 0.5 * (1.0 + tangent) + (0.5 * v) * (1.0 - tangent * tangent) * (
        GELU_C + 3.0 * GELU_C * GELU_A * square
    )


def lanes4(tile):
    return jnp.concatenate([tile] * GRP, axis=1)


def put_stack(dst, index, slab):
    head = lax.broadcasted_iota(jnp.int32, (BLK, SLAB), 1) // HEAD_DIM
    for h in range(GRP):
        dst[index, h * BLK : (h + 1) * BLK, :] = jnp.where(head == h, slab, 0.0).astype(bf16)


def diagonal(wide):
    return jnp.concatenate(
        [
            wide[h * HEAD_DIM : (h + 1) * HEAD_DIM, h * BLK : (h + 1) * BLK]
            for h in range(GRP)
        ],
        axis=0,
    )


def kernel(
    nodes,
    tensors,
    x_hbm,
    og_hbm,
    ag_ref,
    fg_ref,
    wq_hbm,
    wk_hbm,
    wv_hbm,
    wo_hbm,
    wu_hbm,
    wd_hbm,
    nbr_ref,
    cnt_ref,
    nm_hbm,
    out_ref,
    x_ref,
    og_ref,
    wq_ref,
    wk_ref,
    wv_ref,
    wo_ref,
    nm_ref,
    halo,
    n1h,
    qm,
    qmr,
    kown,
    vown,
    ktown,
    vtown,
    khal,
    vhal,
    kthal,
    vthal,
    live,
    vsc,
    vbs,
    vbr,
    wbuf,
    sbuf,
    eown,
    ehal,
    att,
    attt,
    top_one,
    count_one,
    lse,
    lser,
    centre,
    centrer,
    inv_own,
    inv_hal,
    mid,
    n2,
    acc,
    gmr,
    dob,
    dor,
    dom,
    domr,
    prem,
    dq,
    dk,
    dv,
    send,
    recv,
    local,
):
    member = lax.axis_index("member")
    node = lax.axis_index("node")
    tensor = lax.axis_index("tensor")
    total = nodes * tensors
    place = node * tensors + tensor
    has_left = place > 0
    has_right = place < total - 1
    after = lax.rem(place + 1, total)
    before = lax.rem(place + total - 1, total)
    right = (member, after // tensors, lax.rem(after, tensors))
    left = (member, before // tensors, lax.rem(before, tensors))
    up = (member, node, lax.rem(tensor + 1, tensors))
    down = (member, node, lax.rem(tensor + tensors - 1, tensors))
    twin = (1 - member, node, tensor)
    column = lax.rem(node, RING)
    plane = node - column
    east = (member, plane + lax.rem(column + 1, RING), tensor)
    west = (member, plane + lax.rem(column + RING - 1, RING), tensor)

    loads = {}
    for i, (name, src, dst) in enumerate(
        (
            ("wu", wu_hbm, wbuf.at[0, 0]),
            ("wd", wd_hbm, wbuf.at[0, 1]),
            ("x", x_hbm, x_ref),
            ("wk", wk_hbm, wk_ref),
            ("wv", wv_hbm, wv_ref),
            ("wq", wq_hbm, wq_ref),
            ("nm", nm_hbm, nm_ref),
            ("wo", wo_hbm, wo_ref),
            ("og", og_hbm, og_ref),
        )
    ):
        loads[name] = pltpu.make_async_copy(src, dst, local.at[i])
        loads[name].start()

    barrier = pltpu.get_barrier_semaphore()
    for peer in (up, down, east, west, twin):
        pl.semaphore_signal(barrier, inc=1, device_id=peer, device_id_type=MESH)

    @pl.when(has_right)
    def _():
        pl.semaphore_signal(barrier, inc=1, device_id=right, device_id_type=MESH)

    @pl.when(has_left)
    def _():
        pl.semaphore_signal(barrier, inc=1, device_id=left, device_id_type=MESH)

    pl.semaphore_wait(barrier, 5 + has_right.astype(jnp.int32) + has_left.astype(jnp.int32))

    def copy(slot, src, dst, peer):
        return pltpu.make_async_remote_copy(
            src_ref=src,
            dst_ref=dst,
            send_sem=send.at[slot],
            recv_sem=recv.at[slot],
            device_id=peer,
            device_id_type=MESH,
        )

    class Pair:
        def __init__(self, slot, to_right, to_left, dst):
            self.to_right = lambda: copy(slot, to_right, dst.at[0], right)
            self.to_left = lambda: copy(slot + 1, to_left, dst.at[1], left)

        def each(self, right_one, left_one, do):
            @pl.when(right_one)
            def _():
                do(self.to_right())

            @pl.when(left_one)
            def _():
                do(self.to_left())

        def start(self):
            self.each(has_right, has_left, lambda c: c.start())

        def wait_send(self):
            self.each(has_right, has_left, lambda c: c.wait_send())

        def wait_recv(self):
            self.each(has_left, has_right, lambda c: c.wait_recv())

    def quarter(turn, start=0, count=QUART):
        place_x = lax.rem(column + turn + RING, RING)
        return pl.ds(pl.multiple_of(place_x * QUART + start, 64), count)

    def stripe(first, parts, chunk):
        return wbuf.at[pl.ds(first, parts), member, chunk]

    mine = quarter(0)

    class Pull:
        def __init__(self, slot, part, peer):
            self.made = lambda src: copy(slot, src.at[mine], wbuf.at[part, member, mine], peer)

        def start(self):
            @pl.when(member == 0)
            def _():
                self.made(wu_hbm).start()

            @pl.when(member == 1)
            def _():
                self.made(wd_hbm).start()

        def wait_send(self):
            self.made(wu_hbm).wait_send()

        def wait_recv(self):
            self.made(wu_hbm).wait_recv()

    pull_up = Pull(4, 1, up)
    pull_down = Pull(5, 2, down)
    pull_up.start()
    pull_down.start()

    class Halves:
        def __init__(self, slots, src, dst):
            self.parts = [
                Pair(slot, src.at[half], src.at[half], dst.at[:, half])
                for slot, half in zip(slots, (pl.ds(0, 256), pl.ds(256, 256)))
            ]

        def wait_send(self):
            for part in self.parts:
                part.wait_send()

    rows = Halves((0, 24), x_hbm, halo)
    rows.parts[0].start()

    def listed(b, wanted):
        hit = jnp.int32(0)
        for j in range(NBR):
            same = (nbr_ref[b, j] == wanted) & (j < cnt_ref[b])
            hit = hit | same.astype(jnp.int32)
        return jnp.where(hit > 0, 0.0, FAR).astype(f32)

    def valid_row(b, carry):
        for c in range(OWN):
            vsc[b * OWN + c] = listed(b, place * OWN + c)
        for j in range(HWIN):
            e = b + j
            vsc[OWN * OWN + b * HWIN + j] = listed(
                b, place * OWN + jnp.where(e < SPAN, e - SPAN, e - SPAN + OWN)
            )
        return carry

    lax.fori_loop(0, OWN, valid_row, 0)
    for b in range(OWN):
        for e in range(OWN):
            row = b * OWN + e
            base = OWN * OWN + b * HWIN
            low = vsc[base + e - b] if e >= b else jnp.float32(FAR)
            high = vsc[base + SPAN + e - b] if e <= b else jnp.float32(FAR)
            vbs[0, row : row + 1, :] = jnp.full((1, BLK), low, f32)
            vbs[1, row : row + 1, :] = jnp.full((1, BLK), high, f32)
    lists = Pair(2, vbs.at[1], vbs.at[0], vbr)
    lists.start()

    @pl.when(jnp.logical_not(has_left))
    def _():
        vbr[0] = jnp.full(vbr.shape[1:], FAR, f32)
        lser[0] = jnp.zeros(lser.shape[1:], f32)
        centrer[0] = jnp.zeros(centrer.shape[1:], f32)
        halo[0] = jnp.zeros(halo.shape[1:], bf16)
        dor[0] = jnp.zeros(dor.shape[1:], bf16)

    @pl.when(jnp.logical_not(has_right))
    def _():
        vbr[1] = jnp.full(vbr.shape[1:], FAR, f32)
        lser[1] = jnp.zeros(lser.shape[1:], f32)
        centrer[1] = jnp.zeros(centrer.shape[1:], f32)
        halo[1] = jnp.zeros(halo.shape[1:], bf16)
        dor[1] = jnp.zeros(dor.shape[1:], bf16)

    def keys_values(normed, base, k_dst, v_dst, kt_dst, vt_dst):
        count = normed.shape[0]
        base = pl.multiple_of(base, BLK)
        k = dot(normed, wk_ref[...]).astype(bf16)
        v = dot(normed, wv_ref[...]).astype(bf16)
        for g in range(NGRP):
            kg, vg = k[:, g * SLAB : (g + 1) * SLAB], v[:, g * SLAB : (g + 1) * SLAB]
            k_dst[g, pl.ds(base, count), :] = kg
            v_dst[g, pl.ds(base, count), :] = vg
            kt_dst[g, :, pl.ds(base, count)] = kg.T
            vt_dst[g, :, pl.ds(base, count)] = vg.T

    def queries(normed, dst, first):
        q = dot(normed, wq_ref[...]).astype(bf16).astype(f32) * HEAD_DIM ** (-0.5)
        for i in range(normed.shape[0] // BLK):
            for g in range(NGRP):
                put_stack(
                    dst,
                    first + i * NGRP + g,
                    q[i * BLK : (i + 1) * BLK, g * SLAB : (g + 1) * SLAB],
                )

    for name in ("x", "wk", "wv", "wq"):
        loads[name].wait()

    def own_rows(r, carry):
        base = pl.multiple_of(r * 256, 256)
        normed, _ = norm_parts(x_ref[pl.ds(base, 256), :].astype(f32))
        normed = (normed * ag_ref[...]).astype(bf16)
        keys_values(normed, base, kown, vown, ktown, vtown)
        queries(normed, qm, r * 2 * NGRP)
        return carry

    lax.fori_loop(0, 2, own_rows, 0, unroll=True)
    rows.parts[1].start()

    loads["nm"].wait()
    for i in range(OWN + 2 * SPAN):
        e = i if i < OWN else (i - OWN - SPAN if i < OWN + SPAN else i - SPAN)
        block = jnp.clip(place * OWN + e, 0, total * OWN - 1)
        line = jnp.where(nm_ref[pl.ds(block, 1), :] > 0, 0.0, FAR).astype(f32)
        live[i * BLK : (i + 1) * BLK, :] = jnp.broadcast_to(line, (BLK, BLK)).T

    def scores(b, g, blocks, keys, first, flags):
        s = dot_last(keys, qm[b * NGRP + g])
        top = jnp.full((1, STK), 4 * FAR, f32)
        for c in range(blocks):
            bias = live[pl.ds(first + c * BLK, BLK), :] + vsc[flags + c]
            part = s[c * BLK : (c + 1) * BLK, :] + lanes4(bias)
            sbuf[g, c * BLK : (c + 1) * BLK, :] = part
            top = jnp.maximum(top, jnp.max(part, axis=0, keepdims=True))
        return top

    def exponentials(b, g, blocks, top, dst):
        count = jnp.zeros((1, STK), f32)
        for c in range(blocks):
            e = jnp.exp(sbuf[g, c * BLK : (c + 1) * BLK, :] - top)
            count = count + jnp.sum(e, axis=0, keepdims=True)
            dst[b * NGRP + g, c * BLK : (c + 1) * BLK, :] = e.astype(bf16)
        return count

    def per_head(slab, row):
        return jnp.concatenate(
            [
                slab[h * HEAD_DIM : (h + 1) * HEAD_DIM, :] * row[:, h * BLK : (h + 1) * BLK]
                for h in range(GRP)
            ],
            axis=0,
        )

    def forward_own(b, carry):
        tops = [scores(b, g, OWN, kown[g], 0, b * OWN) for g in range(NGRP)]
        counts = [exponentials(b, g, OWN, tops[g], eown) for g in range(NGRP)]
        for g in range(NGRP):
            it = b * NGRP + g
            attt[it] = diagonal(dot(vtown[g], eown[it]))
            top_one[pl.ds(it, 1), :] = tops[g]
            count_one[pl.ds(it, 1), :] = counts[g]
        return carry

    lax.fori_loop(0, OWN, forward_own, 0, unroll=True)

    def hand_over(slot, first, parts, chunk):
        made = copy(slot, stripe(first, parts, chunk), stripe(first, parts, chunk), twin)
        made.start()
        handed.append((made, slot, first, parts, chunk))

    handed = []

    pull_up.wait_recv()
    pull_down.wait_recv()
    half_low, half_high = quarter(0, 0, 64), quarter(0, 64, 64)
    cross_up = copy(6, wbuf.at[1, member, half_low], wbuf.at[3, member, half_low], up)
    cross_down = copy(7, wbuf.at[2, member, half_high], wbuf.at[3, member, half_high], down)
    cross_up.start()
    cross_down.start()
    near_east = copy(8, stripe(1, 2, mine), stripe(1, 2, mine), east)
    near_west = copy(9, stripe(1, 2, mine), stripe(1, 2, mine), west)
    near_east.start()
    near_west.start()
    hand_over(20, 1, 2, mine)

    def halo_rows(r, carry):
        side = lax.rem(r, 2)
        base = pl.multiple_of((r // 2) * 256, 256)
        normed, _ = norm_parts(halo[side, pl.ds(base, 256), :].astype(f32))
        normed = (normed * ag_ref[...]).astype(bf16)
        n1h[side, pl.ds(base, 256), :] = normed
        keys_values(normed, side * SPAN * BLK + base, khal, vhal, kthal, vthal)
        return carry

    for half in range(2):
        rows.parts[half].wait_recv()
        lax.fori_loop(2 * half, 2 * half + 2, halo_rows, 0, unroll=True)

    cross_up.wait_recv()
    cross_down.wait_recv()
    far_east = copy(10, stripe(3, 1, mine), stripe(3, 1, mine), east)
    far_west = copy(17, stripe(3, 1, mine), stripe(3, 1, mine), west)
    far_east.start()
    far_west.start()

    near_east.wait_recv()
    near_west.wait_recv()
    from_west, from_east = quarter(-1, 0, 64), quarter(1, 64, 64)
    on_east = copy(18, stripe(1, 2, from_west), stripe(1, 2, from_west), east)
    on_west = copy(19, stripe(1, 2, from_east), stripe(1, 2, from_east), west)
    on_east.start()
    on_west.start()
    hand_over(23, 1, 2, quarter(-1))
    hand_over(26, 1, 2, quarter(1))

    def window(ref, b, g):
        return ref[g, pl.ds(pl.multiple_of(b * BLK, BLK), HWIN * BLK), :]

    def window_t(ref, b, g):
        return ref[g, :, pl.ds(pl.multiple_of(b * BLK, BLK), HWIN * BLK)]

    def forward_halo(b, carry):
        first = pl.multiple_of(b * BLK, BLK) + OWN * BLK
        tops = [
            scores(b, g, HWIN, window(khal, b, g), first, OWN * OWN + b * HWIN)
            for g in range(NGRP)
        ]
        counts = [exponentials(b, g, HWIN, tops[g], ehal) for g in range(NGRP)]
        for g in range(NGRP):
            it = b * NGRP + g
            far = diagonal(dot(window_t(vthal, b, g), ehal[it]))
            near_top = top_one[pl.ds(it, 1), :]
            top = jnp.maximum(near_top, tops[g])
            near = jnp.exp(near_top - top)
            distant = jnp.exp(tops[g] - top)
            count = count_one[pl.ds(it, 1), :] * near + counts[g] * distant
            inverse = 1.0 / count
            near = near * inverse
            distant = distant * inverse
            mixed = per_head(attt[it], near) + per_head(far, distant)
            attt[it] = mixed
            att[g, pl.ds(pl.multiple_of(b * BLK, BLK), BLK), :] = mixed.T.astype(bf16)
            lse[pl.ds(it, 1), :] = top + jnp.log(count)
            inv_own[pl.ds(it, 1), :] = near
            inv_hal[pl.ds(it, 1), :] = distant
        return carry

    lax.fori_loop(0, OWN, forward_halo, 0, unroll=True)

    levels = Pair(11, lse, lse, lser)
    levels.start()

    far_east.wait_recv()
    far_west.wait_recv()
    last_east = copy(21, stripe(3, 1, from_west), stripe(3, 1, from_west), east)
    last_west = copy(22, stripe(3, 1, from_east), stripe(3, 1, from_east), west)
    last_east.start()
    last_west.start()
    on_east.wait_recv()
    on_west.wait_recv()
    hand_over(27, 1, 2, quarter(2))
    hand_over(28, 3, 1, mine)
    hand_over(29, 3, 1, quarter(-1))
    hand_over(30, 3, 1, quarter(1))

    loads["wo"].wait()

    def middle(r, carry):
        part = pl.ds(pl.multiple_of(r * 256, 256), 256)
        value = x_ref[part, :].astype(f32) + (
            dot(att[0, part, :], wo_ref[0:SLAB, :]) + dot(att[1, part, :], wo_ref[SLAB:, :])
        )
        mid[part, :] = value
        normed, _ = norm_parts(value)
        n2[part, :] = (normed * fg_ref[...]).astype(bf16)
        acc[part, :] = jnp.zeros((256, acc.shape[1]), f32)
        return carry

    lax.fori_loop(0, 2, middle, 0, unroll=True)
    loads["og"].wait()
    loads["wu"].wait()
    loads["wd"].wait()

    def hidden(slot):
        def run(r, carry):
            part = pl.ds(pl.multiple_of(r * 256, 256), 256)
            pre = dot(n2[part, :], wbuf[slot, 0])
            slope = gelu_slope(pre)
            grad = dot_last(og_ref[part, :], wbuf[slot, 1])
            act = (grad * slope).astype(bf16)
            acc[part, :] += dot_last(act, wbuf[slot, 0])
            return carry

        lax.fori_loop(0, 2, run, 0, unroll=True)

    other = 1 - member

    def handed_here(first):
        for _, slot, begin, parts, chunk in handed:
            if begin == first:
                landed = wbuf.at[pl.ds(begin, parts), other, chunk]
                copy(slot, landed, landed, twin).wait_recv()

    hidden(0)
    last_east.wait_recv()
    last_west.wait_recv()
    hand_over(31, 3, 1, quarter(2))
    handed_here(1)
    hidden(1)
    hidden(2)

    def far_queries(r, carry):
        side = r // 2
        base = pl.multiple_of(lax.rem(r, 2) * 256, 256)
        queries(n1h[side, pl.ds(base, 256), :], qmr, r * 2 * NGRP)
        return carry

    lax.fori_loop(0, 4, far_queries, 0, unroll=True)
    handed_here(3)
    hidden(3)

    grads = Halves((13, 32), dob, dor)
    for r in range(2):
        part = slice(r * 256, (r + 1) * 256)
        up_grad = og_ref[part, :].astype(f32)
        normed, inverse = norm_parts(mid[part, :])
        res = up_grad + norm_reverse(acc[part, :], normed, inverse, fg_ref[...])
        gmr[part, :] = res
        res_bf = res.astype(bf16)
        n2[part, :] = res_bf
        dob[part, :] = dot_last(res_bf, wo_ref[...]).astype(bf16)
        grads.parts[r].start()

    for r in range(2):
        part = slice(r * 256, (r + 1) * 256)
        grad_wide = dob[part, :].astype(f32)
        grad_t = dot_last(wo_ref[...], n2[part, :]).astype(bf16).astype(f32)
        for i in range(2):
            for g in range(NGRP):
                it = (r * 2 + i) * NGRP + g
                cols = slice(g * SLAB, (g + 1) * SLAB)
                here = slice(i * BLK, (i + 1) * BLK)
                put_stack(dom, it, grad_wide[here, cols])
                product = grad_t[cols, here] * attt[it]
                centre[it : it + 1, :] = jnp.concatenate(
                    [
                        jnp.sum(
                            product[h * HEAD_DIM : (h + 1) * HEAD_DIM], axis=0, keepdims=True
                        )
                        for h in range(GRP)
                    ],
                    axis=1,
                )

    middles = Pair(15, centre, centre, centrer)
    middles.start()

    dk[...] = jnp.zeros(dk.shape, f32)
    dv[...] = jnp.zeros(dv.shape, f32)

    def backward(b, carry):
        for g in range(NGRP):
            it = b * NGRP + g
            grad_stack = dom[it]
            middle_row = centre[pl.ds(it, 1), :]
            grad_prob = dot_last(vown[g], grad_stack)
            probs = eown[it].astype(f32) * inv_own[pl.ds(it, 1), :]
            grad_score = (probs * (grad_prob - middle_row)).astype(bf16)
            dk[g] += dot(grad_score, qm[it])
            dv[g] += dot(probs.astype(bf16), grad_stack)
            wide = dot(ktown[g], grad_score)
            grad_prob = dot_last(window(vhal, b, g), grad_stack)
            probs = ehal[it].astype(f32) * inv_hal[pl.ds(it, 1), :]
            grad_score = (probs * (grad_prob - middle_row)).astype(bf16)
            wide = wide + dot(window_t(kthal, b, g), grad_score)
            dq[g, pl.ds(pl.multiple_of(b * BLK, BLK), BLK), :] = (
                (diagonal(wide) * HEAD_DIM ** (-0.5)).T.astype(bf16)
            )
        return carry

    lax.fori_loop(0, OWN, backward, 0, unroll=True)

    pairs = []
    for side in range(2):
        begin = 0
        for b in range(OWN):
            first, last = (0, b + 1) if side == 0 else (b, OWN)
            pairs.append((side, b, first, last, begin * BLK))
            begin += last - first
    pairs.sort(key=lambda pair: pair[1])

    lists.wait_recv()
    levels.wait_recv()
    for side, b, first, last, begin in pairs:

        def remote_probs(g, carry, side=side, b=b, first=first, last=last, begin=begin):
            it = b * NGRP + g
            level = lser[side, pl.ds(it, 1), :]
            s = dot_last(kown[g, first * BLK : last * BLK, :], qmr[side * NIT + it])
            for c in range(first, last):
                at = (c - first) * BLK
                row = b * OWN + c
                shift = lanes4(vbr[side, row : row + 1, :]) - level
                bias = lanes4(live[c * BLK : (c + 1) * BLK, :]) + shift
                prem[side, g, begin + at : begin + at + BLK, :] = jnp.exp(
                    s[at : at + BLK, :] + bias
                ).astype(bf16)
            return carry

        lax.fori_loop(0, NGRP, remote_probs, 0, unroll=True)

    middles.wait_recv()
    for half in range(2):
        grads.parts[half].wait_recv()
        for side, b, first, last, begin in pairs[half * OWN : (half + 1) * OWN]:
            for g in range(NGRP):
                it = side * NIT + b * NGRP + g
                put_stack(
                    domr,
                    it,
                    dor[side, b * BLK : (b + 1) * BLK, g * SLAB : (g + 1) * SLAB].astype(f32),
                )
                grad_stack = domr[it]
                own = slice(first * BLK, last * BLK)
                probs = prem[side, g, begin : begin + (last - first) * BLK, :]
                grad_prob = dot_last(vown[g, own, :], grad_stack)
                middle_row = centrer[side, b * NGRP + g : b * NGRP + g + 1, :]
                grad_score = (probs.astype(f32) * (grad_prob - middle_row)).astype(bf16)
                dk[g, own, :] += dot(grad_score, qmr[it])
                dv[g, own, :] += dot(probs, grad_stack)

    def finish(r, carry):
        part = pl.ds(pl.multiple_of(r * 256, 256), 256)
        grad = None
        for g in range(NGRP):
            cols = slice(g * SLAB, (g + 1) * SLAB)
            term = dot_last(dq[g, part, :], wq_ref[:, cols])
            term += dot_last(dk[g, part, :].astype(bf16), wk_ref[:, cols])
            term += dot_last(dv[g, part, :].astype(bf16), wv_ref[:, cols])
            grad = term if grad is None else grad + term
        normed, inverse = norm_parts(x_ref[part, :].astype(f32))
        out_ref[part, :] = (
            gmr[part, :] + norm_reverse(grad, normed, inverse, ag_ref[...])
        ).astype(out_ref.dtype)
        return carry

    lax.fori_loop(0, 2, finish, 0, unroll=True)

    for done in (
        rows,
        lists,
        levels,
        middles,
        grads,
        pull_up,
        pull_down,
        cross_up,
        cross_down,
        near_east,
        near_west,
        far_east,
        far_west,
        on_east,
        on_west,
        last_east,
        last_west,
        *[made for made, *_ in handed],
    ):
        done.wait_send()


def body(nodes, tensors, *args):
    (x, og, ag, fg, wq, wk, wv, wo, wu, wd, nbr, cnt, nm) = args
    rows, width = x.shape
    vm = pl.BlockSpec(memory_space=pltpu.VMEM)
    sm = pl.BlockSpec(memory_space=pltpu.SMEM)
    hbm = pl.BlockSpec(memory_space=pl.ANY)
    V = pltpu.VMEM
    own, hal = OWN * BLK, 2 * SPAN * BLK
    return pl.pallas_call(
        functools.partial(kernel, nodes, tensors),
        out_shape=jax.ShapeDtypeStruct((rows, width), bf16),
        in_specs=[hbm] * 2 + [vm] * 2 + [hbm] * 6 + [sm] * 2 + [hbm],
        out_specs=vm,
        scratch_shapes=[
            V((rows, width), bf16),
            V((rows, width), bf16),
            V((width, width), bf16),
            V((width, width), bf16),
            V((width, width), bf16),
            V((width, width), bf16),
            V(nm.shape, jnp.int32),
            V((2, rows, width), bf16),
            V((2, rows, width), bf16),
            V((NIT, STK, SLAB), bf16),
            V((2 * NIT, STK, SLAB), bf16),
            V((NGRP, own, SLAB), bf16),
            V((NGRP, own, SLAB), bf16),
            V((NGRP, SLAB, own), bf16),
            V((NGRP, SLAB, own), bf16),
            V((NGRP, hal, SLAB), bf16),
            V((NGRP, hal, SLAB), bf16),
            V((NGRP, SLAB, hal), bf16),
            V((NGRP, SLAB, hal), bf16),
            V((own + hal, BLK), f32),
            pltpu.SMEM((OWN * (OWN + HWIN),), f32),
            V((2, OWN * OWN, BLK), f32),
            V((2, OWN * OWN, BLK), f32),
            V((4, 2, width, width), bf16),
            V((NGRP, HWIN * BLK, STK), f32),
            V((NIT, own, STK), bf16),
            V((NIT, HWIN * BLK, STK), bf16),
            V((NGRP, rows, SLAB), bf16),
            V((NIT, SLAB, BLK), f32),
            V((NIT, STK), f32),
            V((NIT, STK), f32),
            V((NIT, STK), f32),
            V((2, NIT, STK), f32),
            V((NIT, STK), f32),
            V((2, NIT, STK), f32),
            V((NIT, STK), f32),
            V((NIT, STK), f32),
            V((rows, width), f32),
            V((rows, width), bf16),
            V((rows, width), f32),
            V((rows, width), f32),
            V((rows, width), bf16),
            V((2, rows, width), bf16),
            V((NIT, STK, SLAB), bf16),
            V((2 * NIT, STK, SLAB), bf16),
            V((2, NGRP, OWN * (OWN + 1) // 2 * BLK, STK), bf16),
            V((NGRP, rows, SLAB), bf16),
            V((NGRP, rows, SLAB), f32),
            V((NGRP, rows, SLAB), f32),
            pltpu.SemaphoreType.DMA((34,)),
            pltpu.SemaphoreType.DMA((34,)),
            pltpu.SemaphoreType.DMA((9,)),
        ],
        compiler_params=pltpu.CompilerParams(
            collective_id=0, has_side_effects=True, vmem_limit_bytes=62 * 1024 * 1024
        ),
    )(x, og, ag.reshape(1, width), fg.reshape(1, width), wq, wk, wv, wo, wu, wd, nbr, cnt, nm)


def solution(mesh):
    return jax.shard_map(
        functools.partial(body, mesh.shape["node"], mesh.shape["tensor"]),
        mesh=mesh,
        in_specs=(
            P(("member", "node", "tensor"), None),
            P(("member", "node", "tensor"), None),
            P(),
            P(),
            P(),
            P(),
            P(),
            P(),
            P(None, "tensor"),
            P("tensor", None),
            P(("node", "tensor"), None),
            P(("node", "tensor")),
            P(),
        ),
        out_specs=P(("member", "node", "tensor"), None),
        check_vma=False,
    )
```

```python
import functools

import jax
import jax.numpy as jnp
from jax import lax
from jax.experimental import pallas as pl
from jax.experimental.pallas import tpu as pltpu
from jax.sharding import PartitionSpec as P

HEADS = 8
HEAD_DIM = 64
NBR = 8
SPAN = 4
BLK = 128
OWN = 4
HWIN = SPAN + 1
GRP = 4
SLAB = GRP * HEAD_DIM
NGRP = HEADS // GRP
STK = GRP * BLK
NIT = OWN * NGRP
RING = 4
QUART = 128

NORM_EPS = 1e-05
GELU_C = 0.7978845608028654
GELU_A = 0.044715
FAR = -1e30

f32 = jnp.float32
bf16 = jnp.bfloat16
MESH = pl.DeviceIdType.MESH


def dot(left, right):
    return jnp.dot(left, right, preferred_element_type=f32)


def dot_last(left, right):
    return lax.dot_general(left, right, (((1,), (1,)), ((), ())), preferred_element_type=f32)


def norm_parts(values):
    centre = jnp.mean(values, axis=-1, keepdims=True)
    centred = values - centre
    inverse = lax.rsqrt(jnp.mean(centred * centred, axis=-1, keepdims=True) + NORM_EPS)
    return centred * inverse, inverse


def norm_reverse(upstream, normed, inverse, gain):
    scaled = upstream * gain
    first = jnp.mean(scaled, axis=-1, keepdims=True)
    second = jnp.mean(scaled * normed, axis=-1, keepdims=True)
    return inverse * (scaled - first - normed * second)


def gelu_slope(v):
    square = v * v
    tangent = jnp.tanh(v * (GELU_C + GELU_C * GELU_A * square))
    return 0.5 * (1.0 + tangent) + (0.5 * v) * (1.0 - tangent * tangent) * (
        GELU_C + 3.0 * GELU_C * GELU_A * square
    )


def lanes4(tile):
    return jnp.concatenate([tile] * GRP, axis=1)


def put_stack(dst, index, slab):
    head = lax.broadcasted_iota(jnp.int32, (BLK, SLAB), 1) // HEAD_DIM
    for h in range(GRP):
        dst[index, h * BLK : (h + 1) * BLK, :] = jnp.where(head == h, slab, 0.0).astype(bf16)


def diagonal(wide):
    return jnp.concatenate(
        [
            wide[h * HEAD_DIM : (h + 1) * HEAD_DIM, h * BLK : (h + 1) * BLK]
            for h in range(GRP)
        ],
        axis=0,
    )


def kernel(
    nodes,
    tensors,
    x_hbm,
    og_hbm,
    ag_ref,
    fg_ref,
    wq_hbm,
    wk_hbm,
    wv_hbm,
    wo_hbm,
    wu_hbm,
    wd_hbm,
    nbr_ref,
    cnt_ref,
    nm_hbm,
    out_ref,
    x_ref,
    og_ref,
    wq_ref,
    wk_ref,
    wv_ref,
    wo_ref,
    nm_ref,
    halo,
    n1h,
    qm,
    qmr,
    kown,
    vown,
    ktown,
    vtown,
    khal,
    vhal,
    kthal,
    vthal,
    live,
    vsc,
    vbs,
    vbr,
    wbuf,
    sbuf,
    eown,
    ehal,
    att,
    attt,
    top_one,
    count_one,
    lse,
    lser,
    centre,
    centrer,
    inv_own,
    inv_hal,
    mid,
    n2,
    acc,
    gmr,
    dob,
    dor,
    dom,
    domr,
    prem,
    dq,
    dk,
    dv,
    send,
    recv,
    local,
):
    member = lax.axis_index("member")
    node = lax.axis_index("node")
    tensor = lax.axis_index("tensor")
    total = nodes * tensors
    place = node * tensors + tensor
    has_left = place > 0
    has_right = place < total - 1
    after = lax.rem(place + 1, total)
    before = lax.rem(place + total - 1, total)
    right = (member, after // tensors, lax.rem(after, tensors))
    left = (member, before // tensors, lax.rem(before, tensors))
    up = (member, node, lax.rem(tensor + 1, tensors))
    down = (member, node, lax.rem(tensor + tensors - 1, tensors))
    twin = (1 - member, node, tensor)
    column = lax.rem(node, RING)
    plane = node - column
    east = (member, plane + lax.rem(column + 1, RING), tensor)
    west = (member, plane + lax.rem(column + RING - 1, RING), tensor)

    loads = {}
    for i, (name, src, dst) in enumerate(
        (
            ("wu", wu_hbm, wbuf.at[0, 0]),
            ("wd", wd_hbm, wbuf.at[0, 1]),
            ("x", x_hbm, x_ref),
            ("wk", wk_hbm, wk_ref),
            ("wv", wv_hbm, wv_ref),
            ("wq", wq_hbm, wq_ref),
            ("nm", nm_hbm, nm_ref),
            ("wo", wo_hbm, wo_ref),
            ("og", og_hbm, og_ref),
        )
    ):
        loads[name] = pltpu.make_async_copy(src, dst, local.at[i])
        loads[name].start()

    barrier = pltpu.get_barrier_semaphore()
    for peer in (up, down, east, west, twin):
        pl.semaphore_signal(barrier, inc=1, device_id=peer, device_id_type=MESH)

    @pl.when(has_right)
    def _():
        pl.semaphore_signal(barrier, inc=1, device_id=right, device_id_type=MESH)

    @pl.when(has_left)
    def _():
        pl.semaphore_signal(barrier, inc=1, device_id=left, device_id_type=MESH)

    pl.semaphore_wait(barrier, 5 + has_right.astype(jnp.int32) + has_left.astype(jnp.int32))

    def copy(slot, src, dst, peer):
        return pltpu.make_async_remote_copy(
            src_ref=src,
            dst_ref=dst,
            send_sem=send.at[slot],
            recv_sem=recv.at[slot],
            device_id=peer,
            device_id_type=MESH,
        )

    class Pair:
        def __init__(self, slot, to_right, to_left, dst):
            self.to_right = lambda: copy(slot, to_right, dst.at[0], right)
            self.to_left = lambda: copy(slot + 1, to_left, dst.at[1], left)

        def each(self, right_one, left_one, do):
            @pl.when(right_one)
            def _():
                do(self.to_right())

            @pl.when(left_one)
            def _():
                do(self.to_left())

        def start(self):
            self.each(has_right, has_left, lambda c: c.start())

        def wait_send(self):
            self.each(has_right, has_left, lambda c: c.wait_send())

        def wait_recv(self):
            self.each(has_left, has_right, lambda c: c.wait_recv())

    def quarter(turn, start=0, count=QUART):
        place_x = lax.rem(column + turn + RING, RING)
        return pl.ds(pl.multiple_of(place_x * QUART + start, 64), count)

    def stripe(first, parts, chunk):
        return wbuf.at[pl.ds(first, parts), member, chunk]

    mine = quarter(0)

    class Pull:
        def __init__(self, slot, part, peer):
            self.made = lambda src: copy(slot, src.at[mine], wbuf.at[part, member, mine], peer)

        def start(self):
            @pl.when(member == 0)
            def _():
                self.made(wu_hbm).start()

            @pl.when(member == 1)
            def _():
                self.made(wd_hbm).start()

        def wait_send(self):
            self.made(wu_hbm).wait_send()

        def wait_recv(self):
            self.made(wu_hbm).wait_recv()

    pull_up = Pull(4, 1, up)
    pull_down = Pull(5, 2, down)
    pull_up.start()
    pull_down.start()

    class Halves:
        def __init__(self, slots, src, dst):
            self.parts = [
                Pair(slot, src.at[half], src.at[half], dst.at[:, half])
                for slot, half in zip(slots, (pl.ds(0, 256), pl.ds(256, 256)))
            ]

        def wait_send(self):
            for part in self.parts:
                part.wait_send()

    rows = Halves((0, 24), x_hbm, halo)
    rows.parts[0].start()

    def listed(b, wanted):
        hit = jnp.int32(0)
        for j in range(NBR):
            same = (nbr_ref[b, j] == wanted) & (j < cnt_ref[b])
            hit = hit | same.astype(jnp.int32)
        return jnp.where(hit > 0, 0.0, FAR).astype(f32)

    def valid_row(b, carry):
        for c in range(OWN):
            vsc[b * OWN + c] = listed(b, place * OWN + c)
        for j in range(HWIN):
            e = b + j
            vsc[OWN * OWN + b * HWIN + j] = listed(
                b, place * OWN + jnp.where(e < SPAN, e - SPAN, e - SPAN + OWN)
            )
        return carry

    lax.fori_loop(0, OWN, valid_row, 0)
    for b in range(OWN):
        for e in range(OWN):
            row = b * OWN + e
            base = OWN * OWN + b * HWIN
            low = vsc[base + e - b] if e >= b else jnp.float32(FAR)
            high = vsc[base + SPAN + e - b] if e <= b else jnp.float32(FAR)
            vbs[0, row : row + 1, :] = jnp.full((1, BLK), low, f32)
            vbs[1, row : row + 1, :] = jnp.full((1, BLK), high, f32)
    lists = Pair(2, vbs.at[1], vbs.at[0], vbr)
    lists.start()

    @pl.when(jnp.logical_not(has_left))
    def _():
        vbr[0] = jnp.full(vbr.shape[1:], FAR, f32)
        lser[0] = jnp.zeros(lser.shape[1:], f32)
        centrer[0] = jnp.zeros(centrer.shape[1:], f32)
        halo[0] = jnp.zeros(halo.shape[1:], bf16)
        dor[0] = jnp.zeros(dor.shape[1:], bf16)

    @pl.when(jnp.logical_not(has_right))
    def _():
        vbr[1] = jnp.full(vbr.shape[1:], FAR, f32)
        lser[1] = jnp.zeros(lser.shape[1:], f32)
        centrer[1] = jnp.zeros(centrer.shape[1:], f32)
        halo[1] = jnp.zeros(halo.shape[1:], bf16)
        dor[1] = jnp.zeros(dor.shape[1:], bf16)

    def keys_values(normed, base, k_dst, v_dst, kt_dst, vt_dst):
        count = normed.shape[0]
        base = pl.multiple_of(base, BLK)
        k = dot(normed, wk_ref[...]).astype(bf16)
        v = dot(normed, wv_ref[...]).astype(bf16)
        for g in range(NGRP):
            kg, vg = k[:, g * SLAB : (g + 1) * SLAB], v[:, g * SLAB : (g + 1) * SLAB]
            k_dst[g, pl.ds(base, count), :] = kg
            v_dst[g, pl.ds(base, count), :] = vg
            kt_dst[g, :, pl.ds(base, count)] = kg.T
            vt_dst[g, :, pl.ds(base, count)] = vg.T

    def queries(normed, dst, first):
        q = dot(normed, wq_ref[...]).astype(bf16).astype(f32) * HEAD_DIM ** (-0.5)
        for i in range(normed.shape[0] // BLK):
            for g in range(NGRP):
                put_stack(
                    dst,
                    first + i * NGRP + g,
                    q[i * BLK : (i + 1) * BLK, g * SLAB : (g + 1) * SLAB],
                )

    for name in ("x", "wk", "wv", "wq"):
        loads[name].wait()

    def own_rows(r, carry):
        base = pl.multiple_of(r * 256, 256)
        normed, _ = norm_parts(x_ref[pl.ds(base, 256), :].astype(f32))
        normed = (normed * ag_ref[...]).astype(bf16)
        keys_values(normed, base, kown, vown, ktown, vtown)
        queries(normed, qm, r * 2 * NGRP)
        return carry

    lax.fori_loop(0, 2, own_rows, 0, unroll=True)
    rows.parts[1].start()

    loads["nm"].wait()
    for i in range(OWN + 2 * SPAN):
        e = i if i < OWN else (i - OWN - SPAN if i < OWN + SPAN else i - SPAN)
        block = jnp.clip(place * OWN + e, 0, total * OWN - 1)
        line = jnp.where(nm_ref[pl.ds(block, 1), :] > 0, 0.0, FAR).astype(f32)
        live[i * BLK : (i + 1) * BLK, :] = jnp.broadcast_to(line, (BLK, BLK)).T

    def scores(b, g, blocks, keys, first, flags):
        s = dot_last(keys, qm[b * NGRP + g])
        top = jnp.full((1, STK), 4 * FAR, f32)
        for c in range(blocks):
            bias = live[pl.ds(first + c * BLK, BLK), :] + vsc[flags + c]
            part = s[c * BLK : (c + 1) * BLK, :] + lanes4(bias)
            sbuf[g, c * BLK : (c + 1) * BLK, :] = part
            top = jnp.maximum(top, jnp.max(part, axis=0, keepdims=True))
        return top

    def exponentials(b, g, blocks, top, dst):
        count = jnp.zeros((1, STK), f32)
        for c in range(blocks):
            e = jnp.exp(sbuf[g, c * BLK : (c + 1) * BLK, :] - top)
            count = count + jnp.sum(e, axis=0, keepdims=True)
            dst[b * NGRP + g, c * BLK : (c + 1) * BLK, :] = e.astype(bf16)
        return count

    def per_head(slab, row):
        return jnp.concatenate(
            [
                slab[h * HEAD_DIM : (h + 1) * HEAD_DIM, :] * row[:, h * BLK : (h + 1) * BLK]
                for h in range(GRP)
            ],
            axis=0,
        )

    def forward_own(b, carry):
        tops = [scores(b, g, OWN, kown[g], 0, b * OWN) for g in range(NGRP)]
        counts = [exponentials(b, g, OWN, tops[g], eown) for g in range(NGRP)]
        for g in range(NGRP):
            it = b * NGRP + g
            attt[it] = diagonal(dot(vtown[g], eown[it]))
            top_one[pl.ds(it, 1), :] = tops[g]
            count_one[pl.ds(it, 1), :] = counts[g]
        return carry

    lax.fori_loop(0, OWN, forward_own, 0, unroll=True)

    def hand_over(slot, first, parts, chunk):
        made = copy(slot, stripe(first, parts, chunk), stripe(first, parts, chunk), twin)
        made.start()
        handed.append((made, slot, first, parts, chunk))

    handed = []

    pull_up.wait_recv()
    pull_down.wait_recv()
    half_low, half_high = quarter(0, 0, 64), quarter(0, 64, 64)
    cross_up = copy(6, wbuf.at[1, member, half_low], wbuf.at[3, member, half_low], up)
    cross_down = copy(7, wbuf.at[2, member, half_high], wbuf.at[3, member, half_high], down)
    cross_up.start()
    cross_down.start()
    near_east = copy(8, stripe(1, 2, mine), stripe(1, 2, mine), east)
    near_west = copy(9, stripe(1, 2, mine), stripe(1, 2, mine), west)
    near_east.start()
    near_west.start()
    hand_over(20, 1, 2, mine)

    def halo_rows(r, carry):
        side = lax.rem(r, 2)
        base = pl.multiple_of((r // 2) * 256, 256)
        normed, _ = norm_parts(halo[side, pl.ds(base, 256), :].astype(f32))
        normed = (normed * ag_ref[...]).astype(bf16)
        n1h[side, pl.ds(base, 256), :] = normed
        keys_values(normed, side * SPAN * BLK + base, khal, vhal, kthal, vthal)
        return carry

    for half in range(2):
        rows.parts[half].wait_recv()
        lax.fori_loop(2 * half, 2 * half + 2, halo_rows, 0, unroll=True)

    cross_up.wait_recv()
    cross_down.wait_recv()
    far_east = copy(10, stripe(3, 1, mine), stripe(3, 1, mine), east)
    far_west = copy(17, stripe(3, 1, mine), stripe(3, 1, mine), west)
    far_east.start()
    far_west.start()

    near_east.wait_recv()
    near_west.wait_recv()
    from_west, from_east = quarter(-1, 0, 64), quarter(1, 64, 64)
    on_east = copy(18, stripe(1, 2, from_west), stripe(1, 2, from_west), east)
    on_west = copy(19, stripe(1, 2, from_east), stripe(1, 2, from_east), west)
    on_east.start()
    on_west.start()
    hand_over(23, 1, 2, quarter(-1))
    hand_over(26, 1, 2, quarter(1))

    def window(ref, b, g):
        return ref[g, pl.ds(pl.multiple_of(b * BLK, BLK), HWIN * BLK), :]

    def window_t(ref, b, g):
        return ref[g, :, pl.ds(pl.multiple_of(b * BLK, BLK), HWIN * BLK)]

    def forward_halo(b, carry):
        first = pl.multiple_of(b * BLK, BLK) + OWN * BLK
        tops = [
            scores(b, g, HWIN, window(khal, b, g), first, OWN * OWN + b * HWIN)
            for g in range(NGRP)
        ]
        counts = [exponentials(b, g, HWIN, tops[g], ehal) for g in range(NGRP)]
        for g in range(NGRP):
            it = b * NGRP + g
            far = diagonal(dot(window_t(vthal, b, g), ehal[it]))
            near_top = top_one[pl.ds(it, 1), :]
            top = jnp.maximum(near_top, tops[g])
            near = jnp.exp(near_top - top)
            distant = jnp.exp(tops[g] - top)
            count = count_one[pl.ds(it, 1), :] * near + counts[g] * distant
            inverse = 1.0 / count
            near = near * inverse
            distant = distant * inverse
            mixed = per_head(attt[it], near) + per_head(far, distant)
            attt[it] = mixed
            att[g, pl.ds(pl.multiple_of(b * BLK, BLK), BLK), :] = mixed.T.astype(bf16)
            lse[pl.ds(it, 1), :] = top + jnp.log(count)
            inv_own[pl.ds(it, 1), :] = near
            inv_hal[pl.ds(it, 1), :] = distant
        return carry

    lax.fori_loop(0, OWN, forward_halo, 0, unroll=True)

    levels = Pair(11, lse, lse, lser)
    levels.start()

    far_east.wait_recv()
    far_west.wait_recv()
    last_east = copy(21, stripe(3, 1, from_west), stripe(3, 1, from_west), east)
    last_west = copy(22, stripe(3, 1, from_east), stripe(3, 1, from_east), west)
    last_east.start()
    last_west.start()
    on_east.wait_recv()
    on_west.wait_recv()
    hand_over(27, 1, 2, quarter(2))
    hand_over(28, 3, 1, mine)
    hand_over(29, 3, 1, quarter(-1))
    hand_over(30, 3, 1, quarter(1))

    loads["wo"].wait()

    def middle(r, carry):
        part = pl.ds(pl.multiple_of(r * 256, 256), 256)
        value = x_ref[part, :].astype(f32) + (
            dot(att[0, part, :], wo_ref[0:SLAB, :]) + dot(att[1, part, :], wo_ref[SLAB:, :])
        )
        mid[part, :] = value
        normed, _ = norm_parts(value)
        n2[part, :] = (normed * fg_ref[...]).astype(bf16)
        acc[part, :] = jnp.zeros((256, acc.shape[1]), f32)
        return carry

    lax.fori_loop(0, 2, middle, 0, unroll=True)
    loads["og"].wait()
    loads["wu"].wait()
    loads["wd"].wait()

    def hidden(slot):
        def run(r, carry):
            part = pl.ds(pl.multiple_of(r * 256, 256), 256)
            pre = dot(n2[part, :], wbuf[slot, 0])
            slope = gelu_slope(pre)
            grad = dot_last(og_ref[part, :], wbuf[slot, 1])
            act = (grad * slope).astype(bf16)
            acc[part, :] += dot_last(act, wbuf[slot, 0])
            return carry

        lax.fori_loop(0, 2, run, 0, unroll=True)

    other = 1 - member

    def handed_here(first):
        for _, slot, begin, parts, chunk in handed:
            if begin == first:
                landed = wbuf.at[pl.ds(begin, parts), other, chunk]
                copy(slot, landed, landed, twin).wait_recv()

    hidden(0)
    handed_here(1)
    hidden(1)
    hidden(2)

    last_east.wait_recv()
    last_west.wait_recv()
    hand_over(31, 3, 1, quarter(2))

    def far_queries(r, carry):
        side = r // 2
        base = pl.multiple_of(lax.rem(r, 2) * 256, 256)
        queries(n1h[side, pl.ds(base, 256), :], qmr, r * 2 * NGRP)
        return carry

    lax.fori_loop(0, 4, far_queries, 0, unroll=True)
    handed_here(3)
    hidden(3)

    grads = Halves((13, 32), dob, dor)
    for r in range(2):
        part = slice(r * 256, (r + 1) * 256)
        up_grad = og_ref[part, :].astype(f32)
        normed, inverse = norm_parts(mid[part, :])
        res = up_grad + norm_reverse(acc[part, :], normed, inverse, fg_ref[...])
        gmr[part, :] = res
        res_bf = res.astype(bf16)
        n2[part, :] = res_bf
        dob[part, :] = dot_last(res_bf, wo_ref[...]).astype(bf16)
        grads.parts[r].start()

    for r in range(2):
        part = slice(r * 256, (r + 1) * 256)
        grad_wide = dob[part, :].astype(f32)
        grad_t = dot_last(wo_ref[...], n2[part, :]).astype(bf16).astype(f32)
        for i in range(2):
            for g in range(NGRP):
                it = (r * 2 + i) * NGRP + g
                cols = slice(g * SLAB, (g + 1) * SLAB)
                here = slice(i * BLK, (i + 1) * BLK)
                put_stack(dom, it, grad_wide[here, cols])
                product = grad_t[cols, here] * attt[it]
                centre[it : it + 1, :] = jnp.concatenate(
                    [
                        jnp.sum(
                            product[h * HEAD_DIM : (h + 1) * HEAD_DIM], axis=0, keepdims=True
                        )
                        for h in range(GRP)
                    ],
                    axis=1,
                )

    middles = Pair(15, centre, centre, centrer)
    middles.start()

    dk[...] = jnp.zeros(dk.shape, f32)
    dv[...] = jnp.zeros(dv.shape, f32)

    def backward(b, carry):
        for g in range(NGRP):
            it = b * NGRP + g
            grad_stack = dom[it]
            middle_row = centre[pl.ds(it, 1), :]
            grad_prob = dot_last(vown[g], grad_stack)
            probs = eown[it].astype(f32) * inv_own[pl.ds(it, 1), :]
            grad_score = (probs * (grad_prob - middle_row)).astype(bf16)
            dk[g] += dot(grad_score, qm[it])
            dv[g] += dot(probs.astype(bf16), grad_stack)
            wide = dot(ktown[g], grad_score)
            grad_prob = dot_last(window(vhal, b, g), grad_stack)
            probs = ehal[it].astype(f32) * inv_hal[pl.ds(it, 1), :]
            grad_score = (probs * (grad_prob - middle_row)).astype(bf16)
            wide = wide + dot(window_t(kthal, b, g), grad_score)
            dq[g, pl.ds(pl.multiple_of(b * BLK, BLK), BLK), :] = (
                (diagonal(wide) * HEAD_DIM ** (-0.5)).T.astype(bf16)
            )
        return carry

    lax.fori_loop(0, OWN, backward, 0, unroll=True)

    pairs = []
    for side in range(2):
        begin = 0
        for b in range(OWN):
            first, last = (0, b + 1) if side == 0 else (b, OWN)
            pairs.append((side, b, first, last, begin * BLK))
            begin += last - first
    pairs.sort(key=lambda pair: pair[1])

    lists.wait_recv()
    levels.wait_recv()
    for side, b, first, last, begin in pairs:

        def remote_probs(g, carry, side=side, b=b, first=first, last=last, begin=begin):
            it = b * NGRP + g
            level = lser[side, pl.ds(it, 1), :]
            s = dot_last(kown[g, first * BLK : last * BLK, :], qmr[side * NIT + it])
            for c in range(first, last):
                at = (c - first) * BLK
                row = b * OWN + c
                shift = lanes4(vbr[side, row : row + 1, :]) - level
                bias = lanes4(live[c * BLK : (c + 1) * BLK, :]) + shift
                prem[side, g, begin + at : begin + at + BLK, :] = jnp.exp(
                    s[at : at + BLK, :] + bias
                ).astype(bf16)
            return carry

        lax.fori_loop(0, NGRP, remote_probs, 0, unroll=True)

    middles.wait_recv()
    for half in range(2):
        grads.parts[half].wait_recv()
        for side, b, first, last, begin in pairs[half * OWN : (half + 1) * OWN]:
            for g in range(NGRP):
                it = side * NIT + b * NGRP + g
                put_stack(
                    domr,
                    it,
                    dor[side, b * BLK : (b + 1) * BLK, g * SLAB : (g + 1) * SLAB].astype(f32),
                )
                grad_stack = domr[it]
                own = slice(first * BLK, last * BLK)
                probs = prem[side, g, begin : begin + (last - first) * BLK, :]
                grad_prob = dot_last(vown[g, own, :], grad_stack)
                middle_row = centrer[side, b * NGRP + g : b * NGRP + g + 1, :]
                grad_score = (probs.astype(f32) * (grad_prob - middle_row)).astype(bf16)
                dk[g, own, :] += dot(grad_score, qmr[it])
                dv[g, own, :] += dot(probs, grad_stack)

    def finish(r, carry):
        part = pl.ds(pl.multiple_of(r * 256, 256), 256)
        grad = None
        for g in range(NGRP):
            cols = slice(g * SLAB, (g + 1) * SLAB)
            term = dot_last(dq[g, part, :], wq_ref[:, cols])
            term += dot_last(dk[g, part, :].astype(bf16), wk_ref[:, cols])
            term += dot_last(dv[g, part, :].astype(bf16), wv_ref[:, cols])
            grad = term if grad is None else grad + term
        normed, inverse = norm_parts(x_ref[part, :].astype(f32))
        out_ref[part, :] = (
            gmr[part, :] + norm_reverse(grad, normed, inverse, ag_ref[...])
        ).astype(out_ref.dtype)
        return carry

    lax.fori_loop(0, 2, finish, 0, unroll=True)

    for done in (
        rows,
        lists,
        levels,
        middles,
        grads,
        pull_up,
        pull_down,
        cross_up,
        cross_down,
        near_east,
        near_west,
        far_east,
        far_west,
        on_east,
        on_west,
        last_east,
        last_west,
        *[made for made, *_ in handed],
    ):
        done.wait_send()


def body(nodes, tensors, *args):
    (x, og, ag, fg, wq, wk, wv, wo, wu, wd, nbr, cnt, nm) = args
    rows, width = x.shape
    vm = pl.BlockSpec(memory_space=pltpu.VMEM)
    sm = pl.BlockSpec(memory_space=pltpu.SMEM)
    hbm = pl.BlockSpec(memory_space=pl.ANY)
    V = pltpu.VMEM
    own, hal = OWN * BLK, 2 * SPAN * BLK
    return pl.pallas_call(
        functools.partial(kernel, nodes, tensors),
        out_shape=jax.ShapeDtypeStruct((rows, width), bf16),
        in_specs=[hbm] * 2 + [vm] * 2 + [hbm] * 6 + [sm] * 2 + [hbm],
        out_specs=vm,
        scratch_shapes=[
            V((rows, width), bf16),
            V((rows, width), bf16),
            V((width, width), bf16),
            V((width, width), bf16),
            V((width, width), bf16),
            V((width, width), bf16),
            V(nm.shape, jnp.int32),
            V((2, rows, width), bf16),
            V((2, rows, width), bf16),
            V((NIT, STK, SLAB), bf16),
            V((2 * NIT, STK, SLAB), bf16),
            V((NGRP, own, SLAB), bf16),
            V((NGRP, own, SLAB), bf16),
            V((NGRP, SLAB, own), bf16),
            V((NGRP, SLAB, own), bf16),
            V((NGRP, hal, SLAB), bf16),
            V((NGRP, hal, SLAB), bf16),
            V((NGRP, SLAB, hal), bf16),
            V((NGRP, SLAB, hal), bf16),
            V((own + hal, BLK), f32),
            pltpu.SMEM((OWN * (OWN + HWIN),), f32),
            V((2, OWN * OWN, BLK), f32),
            V((2, OWN * OWN, BLK), f32),
            V((4, 2, width, width), bf16),
            V((NGRP, HWIN * BLK, STK), f32),
            V((NIT, own, STK), bf16),
            V((NIT, HWIN * BLK, STK), bf16),
            V((NGRP, rows, SLAB), bf16),
            V((NIT, SLAB, BLK), f32),
            V((NIT, STK), f32),
            V((NIT, STK), f32),
            V((NIT, STK), f32),
            V((2, NIT, STK), f32),
            V((NIT, STK), f32),
            V((2, NIT, STK), f32),
            V((NIT, STK), f32),
            V((NIT, STK), f32),
            V((rows, width), f32),
            V((rows, width), bf16),
            V((rows, width), f32),
            V((rows, width), f32),
            V((rows, width), bf16),
            V((2, rows, width), bf16),
            V((NIT, STK, SLAB), bf16),
            V((2 * NIT, STK, SLAB), bf16),
            V((2, NGRP, OWN * (OWN + 1) // 2 * BLK, STK), bf16),
            V((NGRP, rows, SLAB), bf16),
            V((NGRP, rows, SLAB), f32),
            V((NGRP, rows, SLAB), f32),
            pltpu.SemaphoreType.DMA((34,)),
            pltpu.SemaphoreType.DMA((34,)),
            pltpu.SemaphoreType.DMA((9,)),
        ],
        compiler_params=pltpu.CompilerParams(
            collective_id=0, has_side_effects=True, vmem_limit_bytes=62 * 1024 * 1024
        ),
    )(x, og, ag.reshape(1, width), fg.reshape(1, width), wq, wk, wv, wo, wu, wd, nbr, cnt, nm)


def solution(mesh):
    return jax.shard_map(
        functools.partial(body, mesh.shape["node"], mesh.shape["tensor"]),
        mesh=mesh,
        in_specs=(
            P(("member", "node", "tensor"), None),
            P(("member", "node", "tensor"), None),
            P(),
            P(),
            P(),
            P(),
            P(),
            P(),
            P(None, "tensor"),
            P("tensor", None),
            P(("node", "tensor"), None),
            P(("node", "tensor")),
            P(),
        ),
        out_specs=P(("member", "node", "tensor"), None),
        check_vma=False,
    )
```
